32 devices in a mesh: dp: 4 (over y, x), expert: 8 (over z, core).
Axes of the slice: x: 2, y: 2, z: 4, core: 2. Of those that a mesh axis runs over, the one named last changes fastest.
Arguments:
- tokens: bfloat16 [4096, 1024], P(('dp', 'expert')), may hold values from -6 to 6
- expert_ids: int32 [4096, 6], P(('dp', 'expert')), may hold values from 0 to 15, all different within a row; in each aligned block of 128 rows (0 to 127, 128 to 255, ...) at most 49 rows name the same one
- router_gates: float32 [4096, 6], P(('dp', 'expert')), may hold values from 0.05 to 1
- w_in: bfloat16 [16, 2, 704, 1024], P('expert', None, 'dp'), may hold values from -0.1875 to 0.1875
- w_down: bfloat16 [16, 704, 1024], P('expert', 'dp'), may hold values from -0.21875 to 0.21875
- cotangent: bfloat16 [4096, 1024], P(('dp', 'expert')), may hold values from -6 to 6
Outputs:
- layer_output: bfloat16 [4096, 1024], P(('dp', 'expert'))
- token_grads: bfloat16 [4096, 1024], P(('dp', 'expert'))
- gate_grads: float32 [4096, 6], P(('dp', 'expert'))
The draws below stay inside these ranges and needn't reach their ends.
Inputs may be any that keep to these rules, and one draw needn't show every extreme that they name: `expert_ids`: each row names 6 different experts. The rows of one device name no expert more than 49 times, and in every draw some device names some expert exactly 49 times.
All inputs are finite; a program needn't handle non-finite values.
Results may differ from the reference program's by a relative error of at most 0.0064.
Values may be sent and summed in bfloat16 or wider, within the bound.
A program may use at most 64 MiB of HBM per device.

```python
import math
import jax
import jax.numpy as jnp
import numpy as np
from jax import lax

D = 1024
FF = 704
TOPK = 6
TOK_DEV = 128
EXPERTS = 16
CAP = 49
TOKENS = 4096
DEVICES = 32


def level_of(rng, shape, shards, smallest, high):
    def one(axis_at, shards_of):
        heights = jax.random.uniform(jax.random.fold_in(jax.random.fold_in(rng, 6), axis_at), (shards_of,), jnp.float32, smallest / len(shards), high / len(shards))
        return jnp.repeat(jnp.exp(heights), shape[axis_at] // shards_of).reshape((-1,) + (1,) * (len(shape) - axis_at - 1))

    level = one(*shards[0])
    for cut in shards[1:]:
        level = level * one(*cut)
    return level


def shared_out(key, own, number, rows, count, top, most, slope):
    order = jax.random.permutation(key, count)
    packed, common = load_shares(count, rows * top, most, slope, True), load_shares(count, rows * top, most, slope, False)
    places = jnp.arange(count)

    def named(tallies, offset_by):
        used = int((tallies > 0).sum())
        fixed = max(1, used // 4)
        shifted = fixed + (places - fixed + offset_by * (used - fixed)) % max(1, count - fixed)
        return jnp.zeros((count,), jnp.int32).at[order[jnp.where(places < fixed, places, shifted)]].set(jnp.asarray(tallies, jnp.int32))

    tallies = jnp.where(number % 4 == 0, named(packed, number // 4), named(common, number - number // 4 - 1))
    mixed = jax.random.permutation(jax.random.fold_in(own, 3), count)
    giver, sink = mixed[0:count // 2 * 2:2], mixed[1:count // 2 * 2:2]
    margin = jnp.minimum(tallies[giver] - 1, most - tallies[sink]) // 2
    margin = jnp.where((giver == order[0]) | (sink == order[0]) | (tallies[sink] == 0), 0, jnp.maximum(margin, 0))
    shifted = jax.random.randint(jax.random.fold_in(own, 4), (count // 2,), 0, 1 << 20) % (margin + 1)
    tallies = tallies.at[giver].add(-shifted).at[sink].add(shifted)
    members = jnp.searchsorted(jnp.cumsum(tallies), jnp.arange(rows * top), side="right").astype(jnp.int32)
    grid = members.reshape(top, rows).T
    grid = grid[jax.random.permutation(jax.random.fold_in(own, 1), rows)]
    offset_by = jax.random.randint(jax.random.fold_in(own, 2), (rows, 1), 0, top)
    return jnp.take_along_axis(grid, (jnp.arange(top)[None, :] + offset_by) % top, axis=1)


def load_shares(number_of, total, most, lean, full):
    weights = [(1 << 20) // math.isqrt(standing ** lean) + 1 for standing in range(1, number_of + 1)]
    largest = most if full else min(most, max(-(-total // number_of), total * weights[0] // sum(weights)))
    least = 1 if total - largest >= number_of - 1 else 0
    given, spare = [largest] + [least] * (number_of - 1), total - largest - least * (number_of - 1)
    while spare > 0:
        free = [i for i in range(1, number_of) if given[i] < largest] or [i for i in range(1, number_of) if given[i] < most]
        whole, left = sum([weights[i] for i in free]), spare
        for i in free:
            extra = min(most - given[i], max(1, left * weights[i] // whole), spare)
            given[i] = given[i] + extra
            spare = spare - extra
    return np.array(given)


def gaussian(rng, dims, scale, most, pieces=(), kind=jnp.bfloat16):
    drawn = scale * jax.random.normal(rng, dims, jnp.float32)
    if pieces:
        drawn = drawn * level_of(rng, dims, pieces, -0.22, 0.18)
    return jnp.clip(drawn, -most, most).astype(kind)


def setup_inputs(seed: int = 0) -> dict:
    seeds = jax.random.split(jax.random.key(seed), 7)
    tokens = gaussian(seeds[0], (TOKENS, D), 1.0, 6.0, ((0, 32),))
    expert_ids_keys = jax.random.split(jax.random.fold_in(seeds[1], 1), TOKENS // TOK_DEV)
    expert_ids_turns = jax.random.permutation(jax.random.fold_in(seeds[1], 3), TOKENS // TOK_DEV)
    expert_ids = jax.vmap(lambda own, number: shared_out(jax.random.fold_in(seeds[1], 2), own, number, TOK_DEV, EXPERTS, TOPK, CAP, 1))(expert_ids_keys, expert_ids_turns).reshape((TOKENS, TOPK))
    router_gates = jnp.clip(jnp.exp(math.log(1.0) - 2.9957323 * jax.random.uniform(seeds[2], (TOKENS, TOPK), jnp.float32) ** level_of(seeds[2], (TOKENS, TOPK), ((0, 32),), -0.2, 0.2)), 0.05, 1.0)
    w_in = gaussian(seeds[3], (EXPERTS, 2, FF, D), D ** -0.5, 0.1875, ((0, 8), (2, 4)))
    w_down = gaussian(seeds[4], (EXPERTS, FF, D), FF ** -0.5, 0.21875, ((0, 8), (1, 4)))
    cotangent = gaussian(seeds[5], (TOKENS, D), 1.0, 6.0, ((0, 32),))
    return dict(tokens=tokens, expert_ids=expert_ids, router_gates=router_gates, w_in=w_in, w_down=w_down, cotangent=cotangent)


def expert_pass(rows_x, rows_grad, w_gate, w_up, w_out):
    gate_pre = jnp.dot(rows_x, w_gate.T, preferred_element_type=jnp.float32)
    up_pre = jnp.dot(rows_x, w_up.T, preferred_element_type=jnp.float32)
    sigmoid_gate = jax.nn.sigmoid(gate_pre)
    activated = gate_pre * sigmoid_gate
    hidden = (activated * up_pre).astype(jnp.bfloat16)
    expert_out = jnp.dot(hidden, w_out, preferred_element_type=jnp.float32).astype(jnp.bfloat16)
    grad_hidden = jnp.dot(rows_grad, w_out.T, preferred_element_type=jnp.float32)
    grad_up = (grad_hidden * activated).astype(jnp.bfloat16)
    grad_gate = (grad_hidden * up_pre * sigmoid_gate * (1.0 + gate_pre * (1.0 - sigmoid_gate))).astype(jnp.bfloat16)
    expert_grad = jnp.dot(grad_gate, w_gate, preferred_element_type=jnp.float32)
    expert_grad = expert_grad + jnp.dot(grad_up, w_up, preferred_element_type=jnp.float32)
    return expert_out, expert_grad.astype(jnp.bfloat16)


def reference(tokens, expert_ids, router_gates, w_in, w_down, cotangent):
    token_total = tokens.shape[0]
    assign_total = token_total * TOPK
    slot_span = DEVICES * CAP
    flat_ids = expert_ids.reshape(-1).astype(jnp.int32)
    flat_gates = router_gates.reshape(-1)
    sorted_slots = jnp.argsort(flat_ids, stable=True).astype(jnp.int32)
    counts = jnp.zeros((EXPERTS,), jnp.int32).at[flat_ids].add(1)
    offsets = (jnp.cumsum(counts) - counts).astype(jnp.int32)
    padded = jnp.concatenate([sorted_slots, jnp.full((slot_span,), assign_total, jnp.int32)])

    def step(carry, expert):
        out_acc, grad_acc, gate_acc = carry
        picked = lax.dynamic_slice_in_dim(padded, offsets[expert], slot_span)
        is_live = jnp.arange(slot_span, dtype=jnp.int32) < counts[expert]
        picked = jnp.where(is_live, picked, assign_total).astype(jnp.int32)
        token_index = jnp.where(is_live, picked // TOPK, 0).astype(jnp.int32)
        gate_value = jnp.where(is_live, flat_gates[jnp.minimum(picked, assign_total - 1)], jnp.zeros((), router_gates.dtype))
        rows_x = tokens[token_index]
        rows_cot = cotangent[token_index].astype(jnp.float32)
        rows_grad = (gate_value[:, None] * rows_cot).astype(jnp.bfloat16)
        weights = w_in[expert]
        expert_out, expert_grad = expert_pass(rows_x, rows_grad, weights[0], weights[1], w_down[expert])
        out_acc = out_acc.at[token_index].add(gate_value[:, None] * expert_out.astype(jnp.float32))
        grad_acc = grad_acc.at[token_index].add(jnp.where(is_live[:, None], expert_grad.astype(jnp.float32), 0.0))
        gate_acc = gate_acc.at[picked].set(jnp.sum(rows_cot * expert_out.astype(jnp.float32), axis=1))
        return (out_acc, grad_acc, gate_acc), None

    start = (jnp.zeros(tokens.shape, jnp.float32), jnp.zeros(tokens.shape, jnp.float32), jnp.zeros((assign_total + 1,), jnp.float32))
    final, unused = lax.scan(step, start, jnp.arange(EXPERTS, dtype=jnp.int32))
    out_acc, grad_acc, gate_acc = final
    layer_output = out_acc.astype(jnp.bfloat16)
    token_grads = grad_acc.astype(jnp.bfloat16)
    gate_grads = gate_acc[:assign_total].reshape(token_total, TOPK)
    return layer_output, token_grads, gate_grads
```

```python
import jax
import jax.numpy as jnp
from jax import lax
from jax.sharding import PartitionSpec as P


def expert_terms(x, cot, ids, gates, full_in, full_down, first_expert):
    exp_local, _, hidden_width, _ = full_in.shape
    out_sum = jnp.zeros(x.shape, jnp.float32)
    grad_sum = jnp.zeros(x.shape, jnp.float32)
    gate_sum = jnp.zeros(gates.shape, jnp.float32)
    nt = (((1,), (1,)), ((), ()))
    nn = (((1,), (0,)), ((), ()))

    def dot(a, b, dims):
        return lax.dot_general(a, b, dims, preferred_element_type=jnp.float32)

    for e in range(exp_local):
        chosen = ids == first_expert + e
        g = jnp.sum(jnp.where(chosen, gates, 0.0), axis=1, keepdims=True)
        w_pair = full_in[e].reshape(2 * hidden_width, -1)
        both = dot(x, w_pair, nt)
        gate_pre, up_pre = both[:, :hidden_width], both[:, hidden_width:]
        s = jax.nn.sigmoid(gate_pre)
        act = gate_pre * s
        hidden = act * up_pre
        gh = dot(cot, full_down[e], nt)
        gate_sum += jnp.where(chosen, jnp.sum(hidden * gh, axis=1, keepdims=True), 0.0)
        out_sum += dot((hidden * g).astype(jnp.bfloat16), full_down[e], nn)
        gh = gh * g
        grad_up = (gh * act).astype(jnp.bfloat16)
        grad_gate = (gh * up_pre * s * (1.0 + gate_pre * (1.0 - s))).astype(jnp.bfloat16)
        grad_sum += dot(jnp.concatenate([grad_gate, grad_up], axis=1), w_pair, nn)
    return out_sum.astype(jnp.bfloat16), grad_sum.astype(jnp.bfloat16), gate_sum


def body(tokens, expert_ids, router_gates, w_in, w_down, cotangent):
    exp_local = w_in.shape[0]
    first_expert = lax.axis_index("expert") * exp_local
    x = lax.all_gather(tokens, "expert", axis=0, tiled=True)
    cot = lax.all_gather(cotangent, "expert", axis=0, tiled=True)
    ids = lax.all_gather(expert_ids, "expert", axis=0, tiled=True)
    gates = lax.all_gather(router_gates, "expert", axis=0, tiled=True)
    full_in = lax.all_gather(w_in, "dp", axis=2, tiled=True)
    full_down = lax.all_gather(w_down, "dp", axis=1, tiled=True)
    rows = x.shape[0]
    if rows <= 1024:
        out, grad, gate = expert_terms(x, cot, ids, gates, full_in, full_down, first_expert)
    else:
        parts = rows // 512
        out, grad, gate = lax.map(
            lambda a: expert_terms(*a, full_in, full_down, first_expert),
            tuple(v.reshape(parts, 512, v.shape[1]) for v in (x, cot, ids, gates)),
        )
        out, grad, gate = (v.reshape(rows, v.shape[2]) for v in (out, grad, gate))
    return tuple(
        lax.psum_scatter(v, "expert", scatter_dimension=0, tiled=True) for v in (out, grad, gate)
    )


def solution(mesh):
    rows = P(("dp", "expert"), None)
    placed = (rows, rows, rows, P("expert", None, "dp", None), P("expert", "dp", None), rows)
    return jax.shard_map(
        body, mesh=mesh, in_specs=placed, out_specs=(rows, rows, rows), check_vma=False
    )
```

```python
import jax
import jax.numpy as jnp
from jax import lax
from jax.experimental import pallas as pl
from jax.experimental.pallas import tpu as pltpu
from jax.sharding import PartitionSpec as P

MESH = pl.DeviceIdType.MESH


def expert_terms(x, cot, ids, gates, full_in, full_down, first_expert):
    exp_local, _, hidden_width, _ = full_in.shape
    out_sum = jnp.zeros(x.shape, jnp.float32)
    grad_sum = jnp.zeros(x.shape, jnp.float32)
    gate_sum = jnp.zeros(gates.shape, jnp.float32)
    nt = (((1,), (1,)), ((), ()))
    nn = (((1,), (0,)), ((), ()))

    def dot(a, b, dims):
        return lax.dot_general(a, b, dims, preferred_element_type=jnp.float32)

    for e in range(exp_local):
        chosen = ids == first_expert + e
        g = jnp.sum(jnp.where(chosen, gates, 0.0), axis=1, keepdims=True)
        w_pair = full_in[e].reshape(2 * hidden_width, -1)
        both = dot(x, w_pair, nt)
        gate_pre, up_pre = both[:, :hidden_width], both[:, hidden_width:]
        s = jax.nn.sigmoid(gate_pre)
        act = gate_pre * s
        hidden = act * up_pre
        gh = dot(cot, full_down[e], nt)
        gate_sum += jnp.where(chosen, jnp.sum(hidden * gh, axis=1, keepdims=True), 0.0)
        out_sum += dot((hidden * g).astype(jnp.bfloat16), full_down[e], nn)
        gh = gh * g
        grad_up = (gh * act).astype(jnp.bfloat16)
        grad_gate = (gh * up_pre * s * (1.0 + gate_pre * (1.0 - s))).astype(jnp.bfloat16)
        grad_sum += dot(jnp.concatenate([grad_gate, grad_up], axis=1), w_pair, nn)
    return out_sum.astype(jnp.bfloat16), grad_sum.astype(jnp.bfloat16), gate_sum


def body(tokens, expert_ids, router_gates, w_in, w_down, cotangent):
    exp_local = w_in.shape[0]
    first_expert = lax.axis_index("expert") * exp_local
    x = lax.all_gather(tokens, "expert", axis=0, tiled=True)
    cot = lax.all_gather(cotangent, "expert", axis=0, tiled=True)
    ids = lax.all_gather(expert_ids, "expert", axis=0, tiled=True)
    gates = lax.all_gather(router_gates, "expert", axis=0, tiled=True)
    full_in = lax.all_gather(w_in, "dp", axis=2, tiled=True)
    full_down = lax.all_gather(w_down, "dp", axis=1, tiled=True)
    rows = x.shape[0]
    if rows <= 1024:
        out, grad, gate = expert_terms(x, cot, ids, gates, full_in, full_down, first_expert)
    else:
        parts = rows // 512
        out, grad, gate = lax.map(
            lambda a: expert_terms(*a, full_in, full_down, first_expert),
            tuple(v.reshape(parts, 512, v.shape[1]) for v in (x, cot, ids, gates)),
        )
        out, grad, gate = (v.reshape(rows, v.shape[2]) for v in (out, grad, gate))
    return tuple(
        lax.psum_scatter(v, "expert", scatter_dimension=0, tiled=True) for v in (out, grad, gate)
    )


def fused_kernel(
    tok_in, cot_in, gm_in, win_in, wd_in,
    out_ref, grad_ref, gv_ref,
    tok, cot, gm, win, wd, acc, gacc, sibs, sibr, gsibs, gsibr, snd, gsnd, up, dn, gup, gdn,
    load_sem, ag_ss, ag_rs, sg_ss, sg_rs, w_ss, w_rs, f_ss, f_rs, sb_ss, sb_rs, ch_ss, up_rs, dn_rs,
):
    dp, ex = lax.axis_index("dp"), lax.axis_index("expert")
    y, x = dp // 2, dp % 2
    z, c = ex // 2, ex % 2
    dp_x, dp_y = y * 2 + (1 - x), (1 - y) * 2 + x
    sibling = (dp, z * 2 + 1 - c)
    above, below = (dp, ex + 2), (dp, ex - 2)
    x_peer, y_peer = (dp_x, ex), (dp_y, ex)
    levels = tok.shape[0] // 2
    top = levels - 1
    part = win_in.shape[2]
    rows, width = tok_in.shape
    cut = part // 32 * 16 + 16
    has_above, has_below = z < top, z > 0

    barrier = pltpu.get_barrier_semaphore()
    for peer in (sibling, x_peer, y_peer):
        pl.semaphore_signal(barrier, inc=1, device_id=peer, device_id_type=MESH)

    @pl.when(has_above)
    def _():
        pl.semaphore_signal(barrier, inc=1, device_id=above, device_id_type=MESH)

    @pl.when(has_below)
    def _():
        pl.semaphore_signal(barrier, inc=1, device_id=below, device_id_type=MESH)

    pl.semaphore_wait(barrier, 3 + jnp.where(has_above, 1, 0) + jnp.where(has_below, 1, 0))

    def remote(src, dst, ss, rs, peer):
        return pltpu.make_async_remote_copy(
            src_ref=src, dst_ref=dst, send_sem=ss, recv_sem=rs, device_id=peer, device_id_type=MESH
        )

    def unit_rows(s):
        return pl.ds(pl.multiple_of(s * part, 16), part)

    def weights_direct(e, axis):
        peer = (x_peer, y_peer)[axis]
        mine = unit_rows(dp)
        return [
            remote(win_in.at[e], win.at[e, :, mine], w_ss.at[e, axis, 0], w_rs.at[e, axis, 0], peer),
            remote(wd_in.at[e], wd.at[e, mine], w_ss.at[e, axis, 1], w_rs.at[e, axis, 1], peer),
        ]

    def weights_forward(e, axis):
        peer = (x_peer, y_peer)[axis]
        s = (dp_y, dp_x)[axis]
        base = pl.multiple_of(s * part, 16)
        mats = win.at[e, axis, unit_rows(s)]
        down = wd.at[e, pl.ds(base, cut)] if axis == 0 else wd.at[e, pl.ds(base + cut, part - cut)]
        return [
            remote(mats, mats, f_ss.at[e, axis, 0], f_rs.at[e, axis, 0], peer),
            remote(down, down, f_ss.at[e, axis, 1], f_rs.at[e, axis, 1], peer),
        ]

    def token_hop(step, direction, own):
        src = ex + 2 * step if direction else ex - 2 * step
        peer = below if direction else above
        refs = (tok, cot, gm)
        srcs = (tok_in, cot_in, gm_in) if own else [r.at[src] for r in refs]
        return [
            remote(a, r.at[src], ag_ss.at[direction, step, i], ag_rs.at[direction, step, i], peer)
            for i, (a, r) in enumerate(zip(srcs, refs))
        ]

    def token_sibling(level, own=False):
        refs = (tok, cot, gm)
        src = level * 2 + c
        srcs = (tok_in, cot_in, gm_in) if own else [r.at[src] for r in refs]
        return [
            remote(a, r.at[src], sg_ss.at[level, i], sg_rs.at[level, i], sibling)
            for i, (a, r) in enumerate(zip(srcs, refs))
        ]

    def start(copies):
        for copy in copies:
            copy.start()

    def arrived(copies):
        for copy in copies:
            copy.wait_recv()

    def left(copies):
        for copy in copies:
            copy.wait_send()

    start(weights_direct(0, 0) + weights_direct(0, 1))

    @pl.when(has_above)
    def _():
        start(token_hop(0, 0, True))

    @pl.when(has_below)
    def _():
        start(token_hop(0, 1, True))

    start(token_sibling(z, True))
    mine = unit_rows(dp)
    loads = [
        pltpu.make_async_copy(a, b, load_sem.at[i])
        for i, (a, b) in enumerate(
            (
                (tok_in, tok.at[ex]),
                (cot_in, cot.at[ex]),
                (gm_in, gm.at[ex]),
                (win_in, win.at[:, :, mine]),
                (wd_in, wd.at[:, mine]),
            )
        )
    ]
    for load in loads:
        load.start()

    def token_step(step):
        @pl.when(z - step - 1 >= 0)
        def _():
            arrived(token_hop(step, 0, True))
            if step + 1 < top:
                @pl.when(has_above)
                def _():
                    start(token_hop(step + 1, 0, False))
            start(token_sibling(z - step - 1))

        @pl.when(z + step + 1 <= top)
        def _():
            arrived(token_hop(step, 1, True))
            if step + 1 < top:
                @pl.when(has_below)
                def _():
                    start(token_hop(step + 1, 1, False))
            start(token_sibling(z + step + 1))

    def pass_on(e):
        arrived(weights_direct(e, 0))
        start(weights_forward(e, 1))
        arrived(weights_direct(e, 1))
        start(weights_forward(e, 0))

    token_step(0)
    pass_on(0)
    start(weights_direct(1, 0) + weights_direct(1, 1))
    for step in range(1, top):
        token_step(step)
    for load in loads:
        load.wait()

    def sibling_arrival(level, carry):
        arrived(token_sibling(level, True))
        return carry

    lax.fori_loop(0, levels, sibling_arrival, 0)
    arrived(weights_forward(0, 0) + weights_forward(0, 1))

    def nt(a, b):
        return lax.dot_general(a, b, (((1,), (1,)), ((), ())), preferred_element_type=jnp.float32)

    def nn(a, b):
        return lax.dot_general(a, b, (((1,), (0,)), ((), ())), preferred_element_type=jnp.float32)

    def compute(q, e):
        both = pl.ds(q * 2, 2)
        xs = tok[both].reshape(2 * rows, width)
        cs = cot[both].reshape(2 * rows, width)
        gmat = gm[both].reshape(2 * rows, gm.shape[2])
        lane = lax.broadcasted_iota(jnp.int32, gmat.shape, 1)
        here = lane == ex * win.shape[0] + e
        g = jnp.sum(jnp.where(here, gmat, 0.0), axis=1, keepdims=True)
        gate_pre = nt(xs, win[e, 0])
        up_pre = nt(xs, win[e, 1])
        gh = nt(cs, wd[e])
        s = jax.nn.sigmoid(gate_pre)
        act = gate_pre * s
        hidden = act * up_pre
        val = jnp.sum(hidden * gh, axis=1, keepdims=True)
        out = nn((hidden * g).astype(jnp.bfloat16), wd[e])
        gh = gh * g
        grad = nn((gh * up_pre * s * (1.0 + gate_pre * (1.0 - s))).astype(jnp.bfloat16), win[e, 0])
        grad = grad + nn((gh * act).astype(jnp.bfloat16), win[e, 1])
        gval = jnp.where(here & (gmat > 0.0), val, 0.0)
        return (
            out.reshape(2, rows, width),
            grad.reshape(2, rows, width),
            gval.reshape(2, rows, gm.shape[2]),
        )

    def first_expert(q, carry):
        out, grad, gval = compute(q, 0)
        acc[q, :, 0] = out
        acc[q, :, 1] = grad
        gacc[q] = gval
        return carry

    lax.fori_loop(0, levels, first_expert, 0)
    pass_on(1)
    arrived(weights_forward(1, 0) + weights_forward(1, 1))

    def level_at(k):
        tables = ((3, 2, 1, 0), (3, 0, 2, 1), (0, 3, 1, 2), (0, 1, 2, 3))
        if levels == 2:
            tables = ((1, 0), (0, 1))
        q = jnp.int32(0)
        for i, table in enumerate(tables):
            for j, level in enumerate(table):
                q = q + jnp.where((z == i) & (k == j), level, 0)
        return q

    def to_sibling(q):
        return [
            remote(sibs.at[q, h], sibr.at[q, h], sb_ss.at[q, h], sb_rs.at[q, h], sibling) for h in (0, 1)
        ] + [remote(gsibs.at[q], gsibr.at[q], sb_ss.at[q, 2], sb_rs.at[q, 2], sibling)]

    def chain(q, direction):
        peer = below if direction else above
        dst, gdst = (dn, gdn) if direction else (up, gup)
        rs = dn_rs if direction else up_rs
        return [
            remote(snd.at[q, h], dst.at[q, h], ch_ss.at[q, h], rs.at[q, h], peer) for h in (0, 1)
        ] + [remote(gsnd.at[q], gdst.at[q], ch_ss.at[q, 2], rs.at[q, 2], peer)]

    def produce(k):
        q = level_at(k)
        out, grad, gval = compute(q, 1)
        acc[q, :, 0] += out
        acc[q, :, 1] += grad
        gacc[q] += gval
        other = 1 - c
        sibs[q] = acc[q, other].astype(sibs.dtype)
        gsibs[q] = gacc[q, other].T[: gsibs.shape[1]]
        start(to_sibling(q))

    def take(q, direction):
        src, gsrc = (dn, gdn) if direction else (up, gup)
        copies = chain(q, direction)
        for h in (0, 1):
            copies[h].wait_recv()
            acc[q, c, h] += src[q, h].astype(jnp.float32)
        copies[2].wait_recv()
        gsnd[q] += gsrc[q]

    def hand_on(q, direction):
        @pl.when(has_above if direction else has_below)
        def _():
            take(q, direction)

        snd[q] = acc[q, c].astype(snd.dtype)
        start(chain(q, direction))

    def consume(k):
        q = level_at(k)
        arrived(to_sibling(q))
        acc[q, c] += sibr[q].astype(jnp.float32)
        gsnd[q] = gacc[q, c].T[: gsnd.shape[1]] + gsibr[q]

        @pl.when(q > z)
        def _():
            hand_on(q, 0)

        @pl.when(q < z)
        def _():
            hand_on(q, 1)

    def turn(k, carry):
        @pl.when(k < levels)
        def _():
            produce(k)

        @pl.when(k > 0)
        def _():
            consume(k - 1)

        return carry

    lax.fori_loop(0, levels + 1, turn, 0)

    @pl.when(has_below)
    def _():
        take(z, 0)

    @pl.when(has_above)
    def _():
        take(z, 1)

    out_ref[...] = acc[z, c, 0].astype(out_ref.dtype)
    grad_ref[...] = acc[z, c, 1].astype(grad_ref.dtype)
    gv_ref[...] = gsnd[z]

    for e in (0, 1):
        for axis in (0, 1):
            left(weights_direct(e, axis) + weights_forward(e, axis))
    for step in range(top):
        @pl.when(has_above & (z - step >= 0))
        def _():
            left(token_hop(step, 0, True))

        @pl.when(has_below & (z + step <= top))
        def _():
            left(token_hop(step, 1, True))

    def finish(q, carry):
        left(token_sibling(q, True))
        left(to_sibling(q))

        @pl.when(q != z)
        def _():
            left(chain(q, 0))

        return carry

    lax.fori_loop(0, levels, finish, 0)


def fused_body(tokens, expert_ids, router_gates, w_in, w_down, cotangent):
    rows, width = tokens.shape
    members = lax.axis_size("expert")
    exp_local, _, part, _ = w_in.shape
    experts = exp_local * members
    units = part * lax.axis_size("dp")
    levels = members // 2
    bf16, f32 = jnp.bfloat16, jnp.float32
    onehot = expert_ids[:, :, None] == jnp.arange(rows, dtype=jnp.int32)
    gm = jnp.sum(jnp.where(onehot, router_gates[:, :, None], 0.0), axis=1)
    dma = pltpu.SemaphoreType.DMA
    vmem = pl.BlockSpec(memory_space=pltpu.VMEM)
    out, grad, gv = pl.pallas_call(
        fused_kernel,
        out_shape=(
            jax.ShapeDtypeStruct((rows, width), bf16),
            jax.ShapeDtypeStruct((rows, width), bf16),
            jax.ShapeDtypeStruct((experts, rows), f32),
        ),
        in_specs=[pl.BlockSpec(memory_space=pl.ANY)] * 5,
        out_specs=(vmem, vmem, vmem),
        scratch_shapes=[
            pltpu.VMEM((members, rows, width), bf16),
            pltpu.VMEM((members, rows, width), bf16),
            pltpu.VMEM((members, rows, rows), f32),
            pltpu.VMEM((exp_local, 2, units, width), bf16),
            pltpu.VMEM((exp_local, units, width), bf16),
            pltpu.VMEM((levels, 2, 2, rows, width), f32),
            pltpu.VMEM((levels, 2, rows, rows), f32),
            pltpu.VMEM((levels, 2, rows, width), bf16),
            pltpu.VMEM((levels, 2, rows, width), bf16),
            pltpu.VMEM((levels, experts, rows), f32),
            pltpu.VMEM((levels, experts, rows), f32),
            pltpu.VMEM((levels, 2, rows, width), bf16),
            pltpu.VMEM((levels, experts, rows), f32),
            pltpu.VMEM((levels, 2, rows, width), bf16),
            pltpu.VMEM((levels, 2, rows, width), bf16),
            pltpu.VMEM((levels, experts, rows), f32),
            pltpu.VMEM((levels, experts, rows), f32),
            dma((5,)),
            dma((2, levels - 1, 3)),
            dma((2, levels - 1, 3)),
            dma((levels, 3)),
            dma((levels, 3)),
            dma((2, 2, 2)),
            dma((2, 2, 2)),
            dma((2, 2, 2)),
            dma((2, 2, 2)),
            dma((levels, 3)),
            dma((levels, 3)),
            dma((levels, 3)),
            dma((levels, 3)),
            dma((levels, 3)),
        ],
        compiler_params=pltpu.CompilerParams(
            collective_id=0, has_side_effects=True, vmem_limit_bytes=56 * 2**20
        ),
    )(tokens, cotangent, gm, w_in, w_down)
    gate = jnp.sum(jnp.where(onehot[:, :, :experts], gv.T[:, None, :], 0.0), axis=2)
    return out, grad, gate


def solution(mesh):
    rows = P(("dp", "expert"), None)
    placed = (rows, rows, rows, P("expert", None, "dp", None), P("expert", "dp", None), rows)
    fits = mesh.shape["dp"] == 4 and mesh.shape["expert"] in (4, 8)
    return jax.shard_map(
        fused_body if fits else body,
        mesh=mesh, in_specs=placed, out_specs=(rows, rows, rows), check_vma=False,
    )
```

```python
import jax
import jax.numpy as jnp
from jax import lax
from jax.experimental import pallas as pl
from jax.experimental.pallas import tpu as pltpu
from jax.sharding import PartitionSpec as P

MESH = pl.DeviceIdType.MESH


def expert_terms(x, cot, ids, gates, full_in, full_down, first_expert):
    exp_local, _, hidden_width, _ = full_in.shape
    out_sum = jnp.zeros(x.shape, jnp.float32)
    grad_sum = jnp.zeros(x.shape, jnp.float32)
    gate_sum = jnp.zeros(gates.shape, jnp.float32)
    nt = (((1,), (1,)), ((), ()))
    nn = (((1,), (0,)), ((), ()))

    def dot(a, b, dims):
        return lax.dot_general(a, b, dims, preferred_element_type=jnp.float32)

    for e in range(exp_local):
        chosen = ids == first_expert + e
        g = jnp.sum(jnp.where(chosen, gates, 0.0), axis=1, keepdims=True)
        w_pair = full_in[e].reshape(2 * hidden_width, -1)
        both = dot(x, w_pair, nt)
        gate_pre, up_pre = both[:, :hidden_width], both[:, hidden_width:]
        s = jax.nn.sigmoid(gate_pre)
        act = gate_pre * s
        hidden = act * up_pre
        gh = dot(cot, full_down[e], nt)
        gate_sum += jnp.where(chosen, jnp.sum(hidden * gh, axis=1, keepdims=True), 0.0)
        out_sum += dot((hidden * g).astype(jnp.bfloat16), full_down[e], nn)
        gh = gh * g
        grad_up = (gh * act).astype(jnp.bfloat16)
        grad_gate = (gh * up_pre * s * (1.0 + gate_pre * (1.0 - s))).astype(jnp.bfloat16)
        grad_sum += dot(jnp.concatenate([grad_gate, grad_up], axis=1), w_pair, nn)
    return out_sum.astype(jnp.bfloat16), grad_sum.astype(jnp.bfloat16), gate_sum


def body(tokens, expert_ids, router_gates, w_in, w_down, cotangent):
    exp_local = w_in.shape[0]
    first_expert = lax.axis_index("expert") * exp_local
    x = lax.all_gather(tokens, "expert", axis=0, tiled=True)
    cot = lax.all_gather(cotangent, "expert", axis=0, tiled=True)
    ids = lax.all_gather(expert_ids, "expert", axis=0, tiled=True)
    gates = lax.all_gather(router_gates, "expert", axis=0, tiled=True)
    full_in = lax.all_gather(w_in, "dp", axis=2, tiled=True)
    full_down = lax.all_gather(w_down, "dp", axis=1, tiled=True)
    rows = x.shape[0]
    if rows <= 1024:
        out, grad, gate = expert_terms(x, cot, ids, gates, full_in, full_down, first_expert)
    else:
        parts = rows // 512
        out, grad, gate = lax.map(
            lambda a: expert_terms(*a, full_in, full_down, first_expert),
            tuple(v.reshape(parts, 512, v.shape[1]) for v in (x, cot, ids, gates)),
        )
        out, grad, gate = (v.reshape(rows, v.shape[2]) for v in (out, grad, gate))
    return tuple(
        lax.psum_scatter(v, "expert", scatter_dimension=0, tiled=True) for v in (out, grad, gate)
    )


def fused_kernel(
    tok_in, cot_in, ids_in, gates_in, win_in, wd_in,
    out_ref, grad_ref, gv_ref,
    tok, cot, gm, win, wd, acc, gacc, sibs, sibr, gsibs, gsibr, snd, gsnd, up, dn, gup, gdn,
    load_sem, ag_ss, ag_rs, sg_ss, sg_rs, w_ss, w_rs, f_ss, f_rs, sb_ss, sb_rs, ch_ss, up_rs, dn_rs,
):
    dp, ex = lax.axis_index("dp"), lax.axis_index("expert")
    y, x = dp // 2, dp % 2
    z, c = ex // 2, ex % 2
    dp_x, dp_y = y * 2 + (1 - x), (1 - y) * 2 + x
    sibling = (dp, z * 2 + 1 - c)
    above, below = (dp, ex + 2), (dp, ex - 2)
    x_peer, y_peer = (dp_x, ex), (dp_y, ex)
    levels = tok.shape[0] // 2
    top = levels - 1
    part = win_in.shape[2]
    rows, width = tok_in.shape
    cut = part // 32 * 16 + 16
    has_above, has_below = z < top, z > 0

    lane = lax.broadcasted_iota(jnp.int32, (rows, rows), 1)
    choices = ids_in.shape[1]
    gm[ex] = sum(
        jnp.where(lane == ids_in[:, k : k + 1], gates_in[:, k : k + 1], 0.0) for k in range(choices)
    )

    barrier = pltpu.get_barrier_semaphore()
    for peer in (sibling, x_peer, y_peer):
        pl.semaphore_signal(barrier, inc=1, device_id=peer, device_id_type=MESH)

    @pl.when(has_above)
    def _():
        pl.semaphore_signal(barrier, inc=1, device_id=above, device_id_type=MESH)

    @pl.when(has_below)
    def _():
        pl.semaphore_signal(barrier, inc=1, device_id=below, device_id_type=MESH)

    pl.semaphore_wait(barrier, 3 + jnp.where(has_above, 1, 0) + jnp.where(has_below, 1, 0))

    def remote(src, dst, ss, rs, peer):
        return pltpu.make_async_remote_copy(
            src_ref=src, dst_ref=dst, send_sem=ss, recv_sem=rs, device_id=peer, device_id_type=MESH
        )

    def unit_rows(s):
        return pl.ds(pl.multiple_of(s * part, 16), part)

    def weights_direct(e, axis):
        peer = (x_peer, y_peer)[axis]
        mine = unit_rows(dp)
        return [
            remote(win_in.at[e], win.at[e, :, mine], w_ss.at[e, axis, 0], w_rs.at[e, axis, 0], peer),
            remote(wd_in.at[e], wd.at[e, mine], w_ss.at[e, axis, 1], w_rs.at[e, axis, 1], peer),
        ]

    def weights_forward(e, axis):
        peer = (x_peer, y_peer)[axis]
        s = (dp_y, dp_x)[axis]
        base = pl.multiple_of(s * part, 16)
        mats = win.at[e, axis, unit_rows(s)]
        down = wd.at[e, pl.ds(base, cut)] if axis == 0 else wd.at[e, pl.ds(base + cut, part - cut)]
        return [
            remote(mats, mats, f_ss.at[e, axis, 0], f_rs.at[e, axis, 0], peer),
            remote(down, down, f_ss.at[e, axis, 1], f_rs.at[e, axis, 1], peer),
        ]

    def token_hop(step, direction, own):
        src = ex + 2 * step if direction else ex - 2 * step
        peer = below if direction else above
        refs = (tok, cot, gm)
        srcs = (tok_in, cot_in, gm.at[src]) if own else [r.at[src] for r in refs]
        return [
            remote(a, r.at[src], ag_ss.at[direction, step, i], ag_rs.at[direction, step, i], peer)
            for i, (a, r) in enumerate(zip(srcs, refs))
        ]

    def token_sibling(level, own=False):
        refs = (tok, cot, gm)
        src = level * 2 + c
        srcs = (tok_in, cot_in, gm.at[src]) if own else [r.at[src] for r in refs]
        return [
            remote(a, r.at[src], sg_ss.at[level, i], sg_rs.at[level, i], sibling)
            for i, (a, r) in enumerate(zip(srcs, refs))
        ]

    def start(copies):
        for copy in copies:
            copy.start()

    def arrived(copies):
        for copy in copies:
            copy.wait_recv()

    def left(copies):
        for copy in copies:
            copy.wait_send()

    start(weights_direct(0, 0) + weights_direct(0, 1))

    @pl.when(has_above)
    def _():
        start(token_hop(0, 0, True))

    @pl.when(has_below)
    def _():
        start(token_hop(0, 1, True))

    start(token_sibling(z, True))
    mine = unit_rows(dp)
    loads = [
        pltpu.make_async_copy(a, b, load_sem.at[i])
        for i, (a, b) in enumerate(
            (
                (tok_in, tok.at[ex]),
                (cot_in, cot.at[ex]),
                (win_in, win.at[:, :, mine]),
                (wd_in, wd.at[:, mine]),
            )
        )
    ]
    for load in loads:
        load.start()

    def token_step(step):
        @pl.when(z - step - 1 >= 0)
        def _():
            arrived(token_hop(step, 0, True))
            if step + 1 < top:
                @pl.when(has_above)
                def _():
                    start(token_hop(step + 1, 0, False))
            start(token_sibling(z - step - 1))

        @pl.when(z + step + 1 <= top)
        def _():
            arrived(token_hop(step, 1, True))
            if step + 1 < top:
                @pl.when(has_below)
                def _():
                    start(token_hop(step + 1, 1, False))
            start(token_sibling(z + step + 1))

    def pass_on(e):
        arrived(weights_direct(e, 0))
        start(weights_forward(e, 1))
        arrived(weights_direct(e, 1))
        start(weights_forward(e, 0))

    token_step(0)
    pass_on(0)
    start(weights_direct(1, 0) + weights_direct(1, 1))
    for step in range(1, top):
        token_step(step)
    for load in loads:
        load.wait()

    def sibling_arrival(level, carry):
        arrived(token_sibling(level, True))
        return carry

    lax.fori_loop(0, levels, sibling_arrival, 0)
    arrived(weights_forward(0, 0) + weights_forward(0, 1))

    def nt(a, b):
        return lax.dot_general(a, b, (((1,), (1,)), ((), ())), preferred_element_type=jnp.float32)

    def nn(a, b):
        return lax.dot_general(a, b, (((1,), (0,)), ((), ())), preferred_element_type=jnp.float32)

    def compute(q, e, base, size):
        both = pl.ds(q * 2, 2)
        units = pl.ds(pl.multiple_of(base, 16), size)
        xs = tok[both].reshape(2 * rows, width)
        cs = cot[both].reshape(2 * rows, width)
        gmat = gm[both].reshape(2 * rows, rows)
        here = lax.broadcasted_iota(jnp.int32, gmat.shape, 1) == ex * win.shape[0] + e
        g = jnp.sum(jnp.where(here, gmat, 0.0), axis=1, keepdims=True)
        gate_pre = nt(xs, win[e, 0, units])
        up_pre = nt(xs, win[e, 1, units])
        gh = nt(cs, wd[e, units])
        s = jax.nn.sigmoid(gate_pre)
        act = gate_pre * s
        hidden = act * up_pre
        val = jnp.sum(hidden * gh, axis=1, keepdims=True)
        out = nn((hidden * g).astype(jnp.bfloat16), wd[e, units])
        gh = gh * g
        grad_gate = (gh * up_pre * s * (1.0 + gate_pre * (1.0 - s))).astype(jnp.bfloat16)
        grad = nn(grad_gate, win[e, 0, units])
        grad = grad + nn((gh * act).astype(jnp.bfloat16), win[e, 1, units])
        gval = jnp.where(here & (gmat > 0.0), val, 0.0)
        return (
            out.reshape(2, rows, width),
            grad.reshape(2, rows, width),
            gval.reshape(2, rows, rows),
        )

    def add(q, e, base, size):
        out, grad, gval = compute(q, e, base, size)
        acc[q, :, 0] += out
        acc[q, :, 1] += grad
        gacc[q] += gval

    def first_expert(q, carry):
        out, grad, gval = compute(q, 0, 0, win.shape[2])
        acc[q, :, 0] = out
        acc[q, :, 1] = grad
        gacc[q] = gval
        return carry

    def near_units(q, carry):
        add(q, 1, y * 2 * part, 2 * part)
        return carry

    lax.fori_loop(0, levels, first_expert, 0)
    pass_on(1)
    lax.fori_loop(0, levels, near_units, 0)
    arrived(weights_forward(1, 0) + weights_forward(1, 1))

    def level_at(k):
        tables = ((3, 2, 1, 0), (3, 0, 2, 1), (0, 3, 1, 2), (0, 1, 2, 3))
        if levels == 2:
            tables = ((1, 0), (0, 1))
        q = jnp.int32(0)
        for i, table in enumerate(tables):
            for j, level in enumerate(table):
                q = q + jnp.where((z == i) & (k == j), level, 0)
        return q

    def to_sibling(q):
        return [
            remote(sibs.at[q, h], sibr.at[q, h], sb_ss.at[q, h], sb_rs.at[q, h], sibling) for h in (0, 1)
        ] + [remote(gsibs.at[q], gsibr.at[q], sb_ss.at[q, 2], sb_rs.at[q, 2], sibling)]

    def chain(q, direction):
        peer = below if direction else above
        dst, gdst = (dn, gdn) if direction else (up, gup)
        rs = dn_rs if direction else up_rs
        return [
            remote(snd.at[q, h], dst.at[q, h], ch_ss.at[q, h], rs.at[q, h], peer) for h in (0, 1)
        ] + [remote(gsnd.at[q], gdst.at[q], ch_ss.at[q, 2], rs.at[q, 2], peer)]

    def produce(k):
        q = level_at(k)
        add(q, 1, (1 - y) * 2 * part, 2 * part)
        other = 1 - c
        sibs[q] = acc[q, other].astype(sibs.dtype)
        gsibs[q] = gacc[q, other].T[: gsibs.shape[1]]
        start(to_sibling(q))

    def take(q, direction, h):
        src, gsrc = (dn, gdn) if direction else (up, gup)
        copies = chain(q, direction)
        copies[h].wait_recv()
        acc[q, c, h] += src[q, h].astype(jnp.float32)
        if h:
            copies[2].wait_recv()
            gsnd[q] += gsrc[q]

    def hand_on(q, direction, h):
        @pl.when(has_above if direction else has_below)
        def _():
            take(q, direction, h)

        copies = chain(q, direction)
        snd[q, h] = acc[q, c, h].astype(snd.dtype)
        copies[h].start()
        if h:
            copies[2].start()

    def consume(k, h):
        q = level_at(k)
        copies = to_sibling(q)
        copies[h].wait_recv()
        acc[q, c, h] += sibr[q, h].astype(jnp.float32)
        if h:
            copies[2].wait_recv()
            gsnd[q] = gacc[q, c].T[: gsnd.shape[1]] + gsibr[q]

        @pl.when(q > z)
        def _():
            hand_on(q, 0, h)

        @pl.when(q < z)
        def _():
            hand_on(q, 1, h)

    def turn(k, carry):
        produce(k)

        @pl.when(k == 1)
        def _():
            consume(0, 0)
            consume(0, 1)

        return carry

    lax.fori_loop(0, levels, turn, 0)
    if levels == 4:
        for h in (0, 1):
            consume(1, h)
            consume(2, h)
    for h in (0, 1):
        consume(levels - 1, h)

        @pl.when(has_below)
        def _():
            take(z, 0, h)

        @pl.when(has_above)
        def _():
            take(z, 1, h)

    out_ref[...] = acc[z, c, 0].astype(out_ref.dtype)
    grad_ref[...] = acc[z, c, 1].astype(grad_ref.dtype)
    fill = jnp.zeros((rows - gsnd.shape[1], rows), jnp.float32)
    by_expert = jnp.concatenate([gsnd[z], fill], axis=0).T
    gate = jnp.zeros((rows, rows), jnp.float32)
    for k in range(choices):
        one = jnp.sum(jnp.where(lane == ids_in[:, k : k + 1], by_expert, 0.0), axis=1, keepdims=True)
        gate = jnp.where(lane == k, one, gate)
    gv_ref[...] = gate[:, :choices]

    for e in (0, 1):
        for axis in (0, 1):
            left(weights_direct(e, axis) + weights_forward(e, axis))
    for step in range(top):
        @pl.when(has_above & (z - step >= 0))
        def _():
            left(token_hop(step, 0, True))

        @pl.when(has_below & (z + step <= top))
        def _():
            left(token_hop(step, 1, True))

    def finish(q, carry):
        left(token_sibling(q, True))
        left(to_sibling(q))

        @pl.when(q != z)
        def _():
            left(chain(q, 0))

        return carry

    lax.fori_loop(0, levels, finish, 0)


def fused_body(tokens, expert_ids, router_gates, w_in, w_down, cotangent):
    rows, width = tokens.shape
    members = lax.axis_size("expert")
    exp_local, _, part, _ = w_in.shape
    experts = exp_local * members
    units = part * lax.axis_size("dp")
    levels = members // 2
    bf16, f32 = jnp.bfloat16, jnp.float32
    dma = pltpu.SemaphoreType.DMA
    vmem = pl.BlockSpec(memory_space=pltpu.VMEM)
    hbm = pl.BlockSpec(memory_space=pl.ANY)
    return pl.pallas_call(
        fused_kernel,
        out_shape=(
            jax.ShapeDtypeStruct((rows, width), bf16),
            jax.ShapeDtypeStruct((rows, width), bf16),
            jax.ShapeDtypeStruct(router_gates.shape, f32),
        ),
        in_specs=[hbm, hbm, vmem, vmem, hbm, hbm],
        out_specs=(vmem, vmem, vmem),
        scratch_shapes=[
            pltpu.VMEM((members, rows, width), bf16),
            pltpu.VMEM((members, rows, width), bf16),
            pltpu.VMEM((members, rows, rows), f32),
            pltpu.VMEM((exp_local, 2, units, width), bf16),
            pltpu.VMEM((exp_local, units, width), bf16),
            pltpu.VMEM((levels, 2, 2, rows, width), f32),
            pltpu.VMEM((levels, 2, rows, rows), f32),
            pltpu.VMEM((levels, 2, rows, width), bf16),
            pltpu.VMEM((levels, 2, rows, width), bf16),
            pltpu.VMEM((levels, experts, rows), f32),
            pltpu.VMEM((levels, experts, rows), f32),
            pltpu.VMEM((levels, 2, rows, width), bf16),
            pltpu.VMEM((levels, experts, rows), f32),
            pltpu.VMEM((levels, 2, rows, width), bf16),
            pltpu.VMEM((levels, 2, rows, width), bf16),
            pltpu.VMEM((levels, experts, rows), f32),
            pltpu.VMEM((levels, experts, rows), f32),
            dma((4,)),
            dma((2, levels - 1, 3)),
            dma((2, levels - 1, 3)),
            dma((levels, 3)),
            dma((levels, 3)),
            dma((2, 2, 2)),
            dma((2, 2, 2)),
            dma((2, 2, 2)),
            dma((2, 2, 2)),
            dma((levels, 3)),
            dma((levels, 3)),
            dma((levels, 3)),
            dma((levels, 3)),
            dma((levels, 3)),
        ],
        compiler_params=pltpu.CompilerParams(
            collective_id=0, has_side_effects=True, vmem_limit_bytes=56 * 2**20
        ),
    )(tokens, cotangent, expert_ids, router_gates, w_in, w_down)


def solution(mesh):
    rows = P(("dp", "expert"), None)
    placed = (rows, rows, rows, P("expert", None, "dp", None), P("expert", "dp", None), rows)
    fits = mesh.shape["dp"] == 4 and mesh.shape["expert"] in (4, 8)
    return jax.shard_map(
        fused_body if fits else body,
        mesh=mesh, in_specs=placed, out_specs=(rows, rows, rows), check_vma=False,
    )
```

```python
import jax
import jax.numpy as jnp
from jax import lax
from jax.experimental import pallas as pl
from jax.experimental.pallas import tpu as pltpu
from jax.sharding import PartitionSpec as P

MESH = pl.DeviceIdType.MESH


def expert_terms(x, cot, ids, gates, full_in, full_down, first_expert):
    exp_local, _, hidden_width, _ = full_in.shape
    out_sum = jnp.zeros(x.shape, jnp.float32)
    grad_sum = jnp.zeros(x.shape, jnp.float32)
    gate_sum = jnp.zeros(gates.shape, jnp.float32)
    nt = (((1,), (1,)), ((), ()))
    nn = (((1,), (0,)), ((), ()))

    def dot(a, b, dims):
        return lax.dot_general(a, b, dims, preferred_element_type=jnp.float32)

    for e in range(exp_local):
        chosen = ids == first_expert + e
        g = jnp.sum(jnp.where(chosen, gates, 0.0), axis=1, keepdims=True)
        w_pair = full_in[e].reshape(2 * hidden_width, -1)
        both = dot(x, w_pair, nt)
        gate_pre, up_pre = both[:, :hidden_width], both[:, hidden_width:]
        s = jax.nn.sigmoid(gate_pre)
        act = gate_pre * s
        hidden = act * up_pre
        gh = dot(cot, full_down[e], nt)
        gate_sum += jnp.where(chosen, jnp.sum(hidden * gh, axis=1, keepdims=True), 0.0)
        out_sum += dot((hidden * g).astype(jnp.bfloat16), full_down[e], nn)
        gh = gh * g
        grad_up = (gh * act).astype(jnp.bfloat16)
        grad_gate = (gh * up_pre * s * (1.0 + gate_pre * (1.0 - s))).astype(jnp.bfloat16)
        grad_sum += dot(jnp.concatenate([grad_gate, grad_up], axis=1), w_pair, nn)
    return out_sum.astype(jnp.bfloat16), grad_sum.astype(jnp.bfloat16), gate_sum


def body(tokens, expert_ids, router_gates, w_in, w_down, cotangent):
    exp_local = w_in.shape[0]
    first_expert = lax.axis_index("expert") * exp_local
    x = lax.all_gather(tokens, "expert", axis=0, tiled=True)
    cot = lax.all_gather(cotangent, "expert", axis=0, tiled=True)
    ids = lax.all_gather(expert_ids, "expert", axis=0, tiled=True)
    gates = lax.all_gather(router_gates, "expert", axis=0, tiled=True)
    full_in = lax.all_gather(w_in, "dp", axis=2, tiled=True)
    full_down = lax.all_gather(w_down, "dp", axis=1, tiled=True)
    rows = x.shape[0]
    if rows <= 1024:
        out, grad, gate = expert_terms(x, cot, ids, gates, full_in, full_down, first_expert)
    else:
        parts = rows // 512
        out, grad, gate = lax.map(
            lambda a: expert_terms(*a, full_in, full_down, first_expert),
            tuple(v.reshape(parts, 512, v.shape[1]) for v in (x, cot, ids, gates)),
        )
        out, grad, gate = (v.reshape(rows, v.shape[2]) for v in (out, grad, gate))
    return tuple(
        lax.psum_scatter(v, "expert", scatter_dimension=0, tiled=True) for v in (out, grad, gate)
    )


def fused_kernel(
    tok_in, cot_in, ids_in, gates_in, win_in, wd_in,
    out_ref, grad_ref, gv_ref,
    tok, cot, gm, win, wd, acc, gacc, pick, xrow, crow, orow, drow, vrow, sibs, sibr, gsibs, gsibr, snd, gsnd, up, dn, gup, gdn,
    load_sem, ag_ss, ag_rs, sg_ss, sg_rs, w_ss, w_rs, f_ss, f_rs, sb_ss, sb_rs, ch_ss, up_rs, dn_rs,
):
    dp, ex = lax.axis_index("dp"), lax.axis_index("expert")
    y, x = dp // 2, dp % 2
    z, c = ex // 2, ex % 2
    dp_x, dp_y = y * 2 + (1 - x), (1 - y) * 2 + x
    sibling = (dp, z * 2 + 1 - c)
    above, below = (dp, ex + 2), (dp, ex - 2)
    x_peer, y_peer = (dp_x, ex), (dp_y, ex)
    levels = tok.shape[0] // 2
    top = levels - 1
    part = win_in.shape[2]
    rows, width = tok_in.shape
    cut = part // 32 * 16 + 16
    has_above, has_below = z < top, z > 0

    experts, choices = gm.shape[1], ids_in.shape[0]
    expert_row = lax.broadcasted_iota(jnp.int32, (experts, rows), 0)
    gm[ex] = sum(
        jnp.where(expert_row == ids_in[k : k + 1], gates_in[k : k + 1], 0.0) for k in range(choices)
    )

    barrier = pltpu.get_barrier_semaphore()
    for peer in (sibling, x_peer, y_peer):
        pl.semaphore_signal(barrier, inc=1, device_id=peer, device_id_type=MESH)

    @pl.when(has_above)
    def _():
        pl.semaphore_signal(barrier, inc=1, device_id=above, device_id_type=MESH)

    @pl.when(has_below)
    def _():
        pl.semaphore_signal(barrier, inc=1, device_id=below, device_id_type=MESH)

    pl.semaphore_wait(barrier, 3 + jnp.where(has_above, 1, 0) + jnp.where(has_below, 1, 0))

    def remote(src, dst, ss, rs, peer):
        return pltpu.make_async_remote_copy(
            src_ref=src, dst_ref=dst, send_sem=ss, recv_sem=rs, device_id=peer, device_id_type=MESH
        )

    def unit_rows(s):
        return pl.ds(pl.multiple_of(s * part, 16), part)

    def weights_direct(e, axis):
        peer = (x_peer, y_peer)[axis]
        mine = unit_rows(dp)
        return [
            remote(win_in.at[e], win.at[e, :, mine], w_ss.at[e, axis, 0], w_rs.at[e, axis, 0], peer),
            remote(wd_in.at[e], wd.at[e, mine], w_ss.at[e, axis, 1], w_rs.at[e, axis, 1], peer),
        ]

    def weights_forward(e, axis):
        peer = (x_peer, y_peer)[axis]
        s = (dp_y, dp_x)[axis]
        base = pl.multiple_of(s * part, 16)
        mats = win.at[e, axis, unit_rows(s)]
        down = wd.at[e, pl.ds(base, cut)] if axis == 0 else wd.at[e, pl.ds(base + cut, part - cut)]
        return [
            remote(mats, mats, f_ss.at[e, axis, 0], f_rs.at[e, axis, 0], peer),
            remote(down, down, f_ss.at[e, axis, 1], f_rs.at[e, axis, 1], peer),
        ]

    def token_hop(step, direction, own):
        src = ex + 2 * step if direction else ex - 2 * step
        peer = below if direction else above
        refs = (tok, cot, gm)
        srcs = (tok_in, cot_in, gm.at[src]) if own else [r.at[src] for r in refs]
        return [
            remote(a, r.at[src], ag_ss.at[direction, step, i], ag_rs.at[direction, step, i], peer)
            for i, (a, r) in enumerate(zip(srcs, refs))
        ]

    def token_sibling(level, own=False):
        refs = (tok, cot, gm)
        src = level * 2 + c
        srcs = (tok_in, cot_in, gm.at[src]) if own else [r.at[src] for r in refs]
        return [
            remote(a, r.at[src], sg_ss.at[level, i], sg_rs.at[level, i], sibling)
            for i, (a, r) in enumerate(zip(srcs, refs))
        ]

    def start(copies):
        for copy in copies:
            copy.start()

    def arrived(copies):
        for copy in copies:
            copy.wait_recv()

    def left(copies):
        for copy in copies:
            copy.wait_send()

    start(weights_direct(0, 0) + weights_direct(0, 1))

    @pl.when(has_above)
    def _():
        start(token_hop(0, 0, True))

    @pl.when(has_below)
    def _():
        start(token_hop(0, 1, True))

    start(token_sibling(z, True))
    mine = unit_rows(dp)
    loads = [
        pltpu.make_async_copy(a, b, load_sem.at[i])
        for i, (a, b) in enumerate(
            (
                (tok_in, tok.at[ex]),
                (cot_in, cot.at[ex]),
                (win_in, win.at[:, :, mine]),
                (wd_in, wd.at[:, mine]),
            )
        )
    ]
    for load in loads:
        load.start()

    def token_step(step):
        @pl.when(z - step - 1 >= 0)
        def _():
            arrived(token_hop(step, 0, True))
            if step + 1 < top:
                @pl.when(has_above)
                def _():
                    start(token_hop(step + 1, 0, False))
            start(token_sibling(z - step - 1))

        @pl.when(z + step + 1 <= top)
        def _():
            arrived(token_hop(step, 1, True))
            if step + 1 < top:
                @pl.when(has_below)
                def _():
                    start(token_hop(step + 1, 1, False))
            start(token_sibling(z + step + 1))

    def pass_on(e):
        arrived(weights_direct(e, 0))
        start(weights_forward(e, 1))
        arrived(weights_direct(e, 1))
        start(weights_forward(e, 0))

    token_step(0)
    pass_on(0)
    start(weights_direct(1, 0) + weights_direct(1, 1))
    for step in range(1, top):
        token_step(step)
    for load in loads:
        load.wait()

    def sibling_arrival(level, carry):
        arrived(token_sibling(level, True))
        return carry

    lax.fori_loop(0, levels, sibling_arrival, 0)
    def nt(a, b):
        return lax.dot_general(a, b, (((1,), (1,)), ((), ())), preferred_element_type=jnp.float32)

    def nn(a, b):
        return lax.dot_general(a, b, (((1,), (0,)), ((), ())), preferred_element_type=jnp.float32)

    def tn(a, b):
        return lax.dot_general(a, b, (((0,), (0,)), ((), ())), preferred_element_type=jnp.float32)

    slots = pick.shape[2]
    span = (2 * rows, 2 * rows)
    earlier = lax.broadcasted_iota(jnp.int32, span, 0) < lax.broadcasted_iota(jnp.int32, span, 1)
    earlier = jnp.where(earlier, 1.0, 0.0).astype(jnp.bfloat16)
    slot = lax.broadcasted_iota(jnp.int32, (slots, 2 * rows), 0).astype(jnp.float32)

    def gate_line(q, e):
        own = expert_row == ex * win.shape[0] + e
        halves = [jnp.sum(jnp.where(own, gm[q * 2 + d], 0.0), axis=0, keepdims=True) for d in (0, 1)]
        return jnp.concatenate(halves, axis=1)

    def gather(q, carry):
        both = pl.ds(q * 2, 2)
        xs = tok[both].reshape(2 * rows, width)
        cs = cot[both].reshape(2 * rows, width)
        for e in (0, 1):
            chosen = jnp.where(gate_line(q, e) > 0.0, 1.0, 0.0)
            rank = nn(jnp.broadcast_to(chosen, (16, 2 * rows)).astype(jnp.bfloat16), earlier)[:1]
            place = jnp.where((slot == rank) & (chosen > 0.0), 1.0, 0.0).astype(jnp.bfloat16)
            pick[e, q] = place
            xrow[e, q] = nn(place, xs).astype(jnp.bfloat16)
            crow[e, q] = nn(place, cs).astype(jnp.bfloat16)
        return carry

    def gate_rows(e):
        parts = [
            jnp.sum(jnp.where(pick[e, q].astype(jnp.float32) > 0.0, gate_line(q, e), 0.0), axis=1, keepdims=True)
            for q in range(levels)
        ]
        return jnp.concatenate(parts, axis=0)

    def compute(e, base, size, first):
        units = pl.ds(pl.multiple_of(base, 16), size)
        xs = xrow[e].reshape(levels * slots, width)
        cs = crow[e].reshape(levels * slots, width)
        g = gate_rows(e)
        gate_pre = nt(xs, win[e, 0, units])
        up_pre = nt(xs, win[e, 1, units])
        gh = nt(cs, wd[e, units])
        s = jax.nn.sigmoid(gate_pre)
        act = gate_pre * s
        hidden = act * up_pre
        val = jnp.sum(hidden * gh, axis=1, keepdims=True)
        out = nn((hidden * g).astype(jnp.bfloat16), wd[e, units])
        gh = gh * g
        grad_gate = (gh * up_pre * s * (1.0 + gate_pre * (1.0 - s))).astype(jnp.bfloat16)
        grad = nn(grad_gate, win[e, 0, units])
        grad = grad + nn((gh * act).astype(jnp.bfloat16), win[e, 1, units])
        for ref, new in ((orow, out), (drow, grad), (vrow, jnp.broadcast_to(val, (levels * slots, rows)))):
            new = new.reshape(ref.shape)
            if first:
                ref[...] = new
            else:
                ref[...] += new

    def scatter(q, e, first):
        place = pick[e, q]
        out = tn(place, orow[q].astype(jnp.bfloat16)).reshape(2, rows, width)
        grad = tn(place, drow[q].astype(jnp.bfloat16)).reshape(2, rows, width)
        line = jnp.where(place.astype(jnp.float32) > 0.0, vrow[q][:, :1], 0.0)
        line = jnp.sum(line, axis=0, keepdims=True)
        own = expert_row == ex * win.shape[0] + e
        for d in (0, 1):
            gval = jnp.where(own, line[:, d * rows : (d + 1) * rows], 0.0)
            if first:
                acc[q, d, 0] = out[d]
                acc[q, d, 1] = grad[d]
                gacc[q, d] = gval
            else:
                acc[q, d, 0] += out[d]
                acc[q, d, 1] += grad[d]
                gacc[q, d] += gval

    def first_scatter(q, carry):
        scatter(q, 0, True)
        return carry

    lax.fori_loop(0, levels, gather, 0)
    arrived(weights_forward(0, 0) + weights_forward(0, 1))
    compute(0, 0, win.shape[2], True)
    lax.fori_loop(0, levels, first_scatter, 0)
    pass_on(1)
    compute(1, y * 2 * part, 2 * part, True)
    arrived(weights_forward(1, 0) + weights_forward(1, 1))
    compute(1, (1 - y) * 2 * part, 2 * part, False)

    def level_at(k):
        tables = ((3, 2, 1, 0), (3, 0, 2, 1), (0, 3, 1, 2), (0, 1, 2, 3))
        if levels == 2:
            tables = ((1, 0), (0, 1))
        q = jnp.int32(0)
        for i, table in enumerate(tables):
            for j, level in enumerate(table):
                q = q + jnp.where((z == i) & (k == j), level, 0)
        return q

    def to_sibling(q):
        return [
            remote(sibs.at[q, h], sibr.at[q, h], sb_ss.at[q, h], sb_rs.at[q, h], sibling) for h in (0, 1)
        ] + [remote(gsibs.at[q], gsibr.at[q], sb_ss.at[q, 2], sb_rs.at[q, 2], sibling)]

    def chain(q, direction):
        peer = below if direction else above
        dst, gdst = (dn, gdn) if direction else (up, gup)
        rs = dn_rs if direction else up_rs
        return [
            remote(snd.at[q, h], dst.at[q, h], ch_ss.at[q, h], rs.at[q, h], peer) for h in (0, 1)
        ] + [remote(gsnd.at[q], gdst.at[q], ch_ss.at[q, 2], rs.at[q, 2], peer)]

    def produce(k):
        q = level_at(k)
        scatter(q, 1, False)
        other = 1 - c
        sibs[q] = acc[q, other].astype(sibs.dtype)
        gsibs[q] = gacc[q, other]
        start(to_sibling(q))

    def take(q, direction, h):
        src, gsrc = (dn, gdn) if direction else (up, gup)
        copies = chain(q, direction)
        copies[h].wait_recv()
        acc[q, c, h] += src[q, h].astype(jnp.float32)
        if h:
            copies[2].wait_recv()
            gsnd[q] += gsrc[q]

    def hand_on(q, direction, h):
        @pl.when(has_above if direction else has_below)
        def _():
            take(q, direction, h)

        copies = chain(q, direction)
        snd[q, h] = acc[q, c, h].astype(snd.dtype)
        copies[h].start()
        if h:
            copies[2].start()

    def consume(k, h):
        q = level_at(k)
        copies = to_sibling(q)
        copies[h].wait_recv()
        acc[q, c, h] += sibr[q, h].astype(jnp.float32)
        if h:
            copies[2].wait_recv()
            gsnd[q] = gacc[q, c] + gsibr[q]

        @pl.when(q > z)
        def _():
            hand_on(q, 0, h)

        @pl.when(q < z)
        def _():
            hand_on(q, 1, h)

    def turn(k, carry):
        produce(k)

        @pl.when(k == 1)
        def _():
            consume(0, 0)
            consume(0, 1)

        return carry

    lax.fori_loop(0, levels, turn, 0)
    if levels == 4:
        for h in (0, 1):
            consume(1, h)
            consume(2, h)
    for h in (0, 1):
        consume(levels - 1, h)

        @pl.when(has_below)
        def _():
            take(z, 0, h)

        @pl.when(has_above)
        def _():
            take(z, 1, h)

    out_ref[...] = acc[z, c, 0].astype(out_ref.dtype)
    grad_ref[...] = acc[z, c, 1].astype(grad_ref.dtype)
    for k in range(choices):
        named = expert_row == ids_in[k : k + 1]
        gv_ref[k : k + 1] = jnp.sum(jnp.where(named, gsnd[z], 0.0), axis=0, keepdims=True)

    for e in (0, 1):
        for axis in (0, 1):
            left(weights_direct(e, axis) + weights_forward(e, axis))
    for step in range(top):
        @pl.when(has_above & (z - step >= 0))
        def _():
            left(token_hop(step, 0, True))

        @pl.when(has_below & (z + step <= top))
        def _():
            left(token_hop(step, 1, True))

    def finish(q, carry):
        left(token_sibling(q, True))
        left(to_sibling(q))

        @pl.when(q != z)
        def _():
            left(chain(q, 0))

        return carry

    lax.fori_loop(0, levels, finish, 0)


def fused_body(tokens, expert_ids, router_gates, w_in, w_down, cotangent):
    rows, width = tokens.shape
    members = lax.axis_size("expert")
    exp_local, _, part, _ = w_in.shape
    experts = exp_local * members
    units = part * lax.axis_size("dp")
    levels = members // 2
    choices = expert_ids.shape[1]
    capacity = rows * choices // experts + 1
    slots = -(-2 * capacity // 16) * 16
    bf16, f32 = jnp.bfloat16, jnp.float32
    dma = pltpu.SemaphoreType.DMA
    vmem = pl.BlockSpec(memory_space=pltpu.VMEM)
    hbm = pl.BlockSpec(memory_space=pl.ANY)
    out, grad, gate = pl.pallas_call(
        fused_kernel,
        out_shape=(
            jax.ShapeDtypeStruct((rows, width), bf16),
            jax.ShapeDtypeStruct((rows, width), bf16),
            jax.ShapeDtypeStruct((choices, rows), f32),
        ),
        in_specs=[hbm, hbm, vmem, vmem, hbm, hbm],
        out_specs=(vmem, vmem, vmem),
        scratch_shapes=[
            pltpu.VMEM((members, rows, width), bf16),
            pltpu.VMEM((members, rows, width), bf16),
            pltpu.VMEM((members, experts, rows), f32),
            pltpu.VMEM((exp_local, 2, units, width), bf16),
            pltpu.VMEM((exp_local, units, width), bf16),
            pltpu.VMEM((levels, 2, 2, rows, width), f32),
            pltpu.VMEM((levels, 2, experts, rows), f32),
            pltpu.VMEM((exp_local, levels, slots, 2 * rows), bf16),
            pltpu.VMEM((exp_local, levels, slots, width), bf16),
            pltpu.VMEM((exp_local, levels, slots, width), bf16),
            pltpu.VMEM((levels, slots, width), f32),
            pltpu.VMEM((levels, slots, width), f32),
            pltpu.VMEM((levels, slots, rows), f32),
            pltpu.VMEM((levels, 2, rows, width), bf16),
            pltpu.VMEM((levels, 2, rows, width), bf16),
            pltpu.VMEM((levels, experts, rows), f32),
            pltpu.VMEM((levels, experts, rows), f32),
            pltpu.VMEM((levels, 2, rows, width), bf16),
            pltpu.VMEM((levels, experts, rows), f32),
            pltpu.VMEM((levels, 2, rows, width), bf16),
            pltpu.VMEM((levels, 2, rows, width), bf16),
            pltpu.VMEM((levels, experts, rows), f32),
            pltpu.VMEM((levels, experts, rows), f32),
            dma((4,)),
            dma((2, levels - 1, 3)),
            dma((2, levels - 1, 3)),
            dma((levels, 3)),
            dma((levels, 3)),
            dma((2, 2, 2)),
            dma((2, 2, 2)),
            dma((2, 2, 2)),
            dma((2, 2, 2)),
            dma((levels, 3)),
            dma((levels, 3)),
            dma((levels, 3)),
            dma((levels, 3)),
            dma((levels, 3)),
        ],
        compiler_params=pltpu.CompilerParams(
            collective_id=0, has_side_effects=True, vmem_limit_bytes=56 * 2**20
        ),
    )(tokens, cotangent, expert_ids.T, router_gates.T, w_in, w_down)
    return out, grad, gate.T


def solution(mesh):
    rows = P(("dp", "expert"), None)
    placed = (rows, rows, rows, P("expert", None, "dp", None), P("expert", "dp", None), rows)
    fits = mesh.shape["dp"] == 4 and mesh.shape["expert"] in (4, 8)
    return jax.shard_map(
        fused_body if fits else body,
        mesh=mesh, in_specs=placed, out_specs=(rows, rows, rows), check_vma=False,
    )
```

```python
import jax
import jax.numpy as jnp
from jax import lax
from jax.experimental import pallas as pl
from jax.experimental.pallas import tpu as pltpu
from jax.sharding import PartitionSpec as P

MESH = pl.DeviceIdType.MESH


def expert_terms(x, cot, ids, gates, full_in, full_down, first_expert):
    exp_local, _, hidden_width, _ = full_in.shape
    out_sum = jnp.zeros(x.shape, jnp.float32)
    grad_sum = jnp.zeros(x.shape, jnp.float32)
    gate_sum = jnp.zeros(gates.shape, jnp.float32)
    nt = (((1,), (1,)), ((), ()))
    nn = (((1,), (0,)), ((), ()))

    def dot(a, b, dims):
        return lax.dot_general(a, b, dims, preferred_element_type=jnp.float32)

    for e in range(exp_local):
        chosen = ids == first_expert + e
        g = jnp.sum(jnp.where(chosen, gates, 0.0), axis=1, keepdims=True)
        w_pair = full_in[e].reshape(2 * hidden_width, -1)
        both = dot(x, w_pair, nt)
        gate_pre, up_pre = both[:, :hidden_width], both[:, hidden_width:]
        s = jax.nn.sigmoid(gate_pre)
        act = gate_pre * s
        hidden = act * up_pre
        gh = dot(cot, full_down[e], nt)
        gate_sum += jnp.where(chosen, jnp.sum(hidden * gh, axis=1, keepdims=True), 0.0)
        out_sum += dot((hidden * g).astype(jnp.bfloat16), full_down[e], nn)
        gh = gh * g
        grad_up = (gh * act).astype(jnp.bfloat16)
        grad_gate = (gh * up_pre * s * (1.0 + gate_pre * (1.0 - s))).astype(jnp.bfloat16)
        grad_sum += dot(jnp.concatenate([grad_gate, grad_up], axis=1), w_pair, nn)
    return out_sum.astype(jnp.bfloat16), grad_sum.astype(jnp.bfloat16), gate_sum


def body(tokens, expert_ids, router_gates, w_in, w_down, cotangent):
    exp_local = w_in.shape[0]
    first_expert = lax.axis_index("expert") * exp_local
    x = lax.all_gather(tokens, "expert", axis=0, tiled=True)
    cot = lax.all_gather(cotangent, "expert", axis=0, tiled=True)
    ids = lax.all_gather(expert_ids, "expert", axis=0, tiled=True)
    gates = lax.all_gather(router_gates, "expert", axis=0, tiled=True)
    full_in = lax.all_gather(w_in, "dp", axis=2, tiled=True)
    full_down = lax.all_gather(w_down, "dp", axis=1, tiled=True)
    rows = x.shape[0]
    if rows <= 1024:
        out, grad, gate = expert_terms(x, cot, ids, gates, full_in, full_down, first_expert)
    else:
        parts = rows // 512
        out, grad, gate = lax.map(
            lambda a: expert_terms(*a, full_in, full_down, first_expert),
            tuple(v.reshape(parts, 512, v.shape[1]) for v in (x, cot, ids, gates)),
        )
        out, grad, gate = (v.reshape(rows, v.shape[2]) for v in (out, grad, gate))
    return tuple(
        lax.psum_scatter(v, "expert", scatter_dimension=0, tiled=True) for v in (out, grad, gate)
    )


def fused_kernel(
    tok_in, cot_in, ids_in, gates_in, win_in, wd_in,
    out_ref, grad_ref, gv_ref,
    tok, cot, gm, win, wd, acc, gacc, pick, xrow, crow, orow, drow, vrow, sibs, sibr, gsibs, gsibr, snd, gsnd, up, dn, gup, gdn,
    load_sem, ag_ss, ag_rs, sg_ss, sg_rs, w_ss, w_rs, f_ss, f_rs, sb_ss, sb_rs, ch_ss, up_rs, dn_rs,
):
    dp, ex = lax.axis_index("dp"), lax.axis_index("expert")
    y, x = dp // 2, dp % 2
    z, c = ex // 2, ex % 2
    dp_x, dp_y = y * 2 + (1 - x), (1 - y) * 2 + x
    sibling = (dp, z * 2 + 1 - c)
    above, below = (dp, ex + 2), (dp, ex - 2)
    x_peer, y_peer = (dp_x, ex), (dp_y, ex)
    levels = tok.shape[0] // 2
    top = levels - 1
    part = win_in.shape[2]
    rows, width = tok_in.shape
    cut = part // 32 * 16 + 16
    has_above, has_below = z < top, z > 0

    experts, choices = gm.shape[1], ids_in.shape[0]
    expert_row = lax.broadcasted_iota(jnp.int32, (experts, rows), 0)
    gm[ex] = sum(
        jnp.where(expert_row == ids_in[k : k + 1], gates_in[k : k + 1], 0.0) for k in range(choices)
    )

    barrier = pltpu.get_barrier_semaphore()
    for peer in (sibling, x_peer, y_peer):
        pl.semaphore_signal(barrier, inc=1, device_id=peer, device_id_type=MESH)

    @pl.when(has_above)
    def _():
        pl.semaphore_signal(barrier, inc=1, device_id=above, device_id_type=MESH)

    @pl.when(has_below)
    def _():
        pl.semaphore_signal(barrier, inc=1, device_id=below, device_id_type=MESH)

    pl.semaphore_wait(barrier, 3 + jnp.where(has_above, 1, 0) + jnp.where(has_below, 1, 0))

    def remote(src, dst, ss, rs, peer):
        return pltpu.make_async_remote_copy(
            src_ref=src, dst_ref=dst, send_sem=ss, recv_sem=rs, device_id=peer, device_id_type=MESH
        )

    def unit_rows(s):
        return pl.ds(pl.multiple_of(s * part, 16), part)

    def weights_direct(e, axis):
        peer = (x_peer, y_peer)[axis]
        mine = unit_rows(dp)
        return [
            remote(win_in.at[e], win.at[e, :, mine], w_ss.at[e, axis, 0], w_rs.at[e, axis, 0], peer),
            remote(wd_in.at[e], wd.at[e, mine], w_ss.at[e, axis, 1], w_rs.at[e, axis, 1], peer),
        ]

    def weights_forward(e, axis):
        peer = (x_peer, y_peer)[axis]
        s = (dp_y, dp_x)[axis]
        base = pl.multiple_of(s * part, 16)
        mats = win.at[e, axis, unit_rows(s)]
        down = wd.at[e, pl.ds(base, cut)] if axis == 0 else wd.at[e, pl.ds(base + cut, part - cut)]
        return [
            remote(mats, mats, f_ss.at[e, axis, 0], f_rs.at[e, axis, 0], peer),
            remote(down, down, f_ss.at[e, axis, 1], f_rs.at[e, axis, 1], peer),
        ]

    def token_hop(step, direction, own):
        src = ex + 2 * step if direction else ex - 2 * step
        peer = below if direction else above
        refs = (tok, cot, gm)
        srcs = (tok_in, cot_in, gm.at[src]) if own else [r.at[src] for r in refs]
        return [
            remote(a, r.at[src], ag_ss.at[direction, step, i], ag_rs.at[direction, step, i], peer)
            for i, (a, r) in enumerate(zip(srcs, refs))
        ]

    def token_sibling(level, own=False):
        refs = (tok, cot, gm)
        src = level * 2 + c
        srcs = (tok_in, cot_in, gm.at[src]) if own else [r.at[src] for r in refs]
        return [
            remote(a, r.at[src], sg_ss.at[level, i], sg_rs.at[level, i], sibling)
            for i, (a, r) in enumerate(zip(srcs, refs))
        ]

    def start(copies):
        for copy in copies:
            copy.start()

    def arrived(copies):
        for copy in copies:
            copy.wait_recv()

    def left(copies):
        for copy in copies:
            copy.wait_send()

    start(weights_direct(0, 0) + weights_direct(0, 1))

    @pl.when(has_above)
    def _():
        start(token_hop(0, 0, True))

    @pl.when(has_below)
    def _():
        start(token_hop(0, 1, True))

    start(token_sibling(z, True))
    mine = unit_rows(dp)
    loads = [
        pltpu.make_async_copy(a, b, load_sem.at[i])
        for i, (a, b) in enumerate(
            (
                (tok_in, tok.at[ex]),
                (cot_in, cot.at[ex]),
                (win_in, win.at[:, :, mine]),
                (wd_in, wd.at[:, mine]),
            )
        )
    ]
    for load in loads:
        load.start()

    def token_step(step):
        @pl.when(z - step - 1 >= 0)
        def _():
            arrived(token_hop(step, 0, True))
            if step + 1 < top:
                @pl.when(has_above)
                def _():
                    start(token_hop(step + 1, 0, False))
            start(token_sibling(z - step - 1))

        @pl.when(z + step + 1 <= top)
        def _():
            arrived(token_hop(step, 1, True))
            if step + 1 < top:
                @pl.when(has_below)
                def _():
                    start(token_hop(step + 1, 1, False))
            start(token_sibling(z + step + 1))

    def pass_on(e):
        arrived(weights_direct(e, 0))
        start(weights_forward(e, 1))
        arrived(weights_direct(e, 1))
        start(weights_forward(e, 0))

    token_step(0)
    start(weights_direct(1, 0) + weights_direct(1, 1))
    pass_on(0)
    for step in range(1, top):
        token_step(step)
    for load in loads:
        load.wait()

    def sibling_arrival(level, carry):
        arrived(token_sibling(level, True))
        return carry

    lax.fori_loop(0, levels, sibling_arrival, 0)
    def nt(a, b):
        return lax.dot_general(a, b, (((1,), (1,)), ((), ())), preferred_element_type=jnp.float32)

    def nn(a, b):
        return lax.dot_general(a, b, (((1,), (0,)), ((), ())), preferred_element_type=jnp.float32)

    def tn(a, b):
        return lax.dot_general(a, b, (((0,), (0,)), ((), ())), preferred_element_type=jnp.float32)

    slots = pick.shape[2]
    span = (2 * rows, 2 * rows)
    earlier = lax.broadcasted_iota(jnp.int32, span, 0) < lax.broadcasted_iota(jnp.int32, span, 1)
    earlier = jnp.where(earlier, 1.0, 0.0).astype(jnp.bfloat16)
    slot = lax.broadcasted_iota(jnp.int32, (slots, 2 * rows), 0).astype(jnp.float32)

    def gate_line(q, e):
        own = expert_row == ex * win.shape[0] + e
        halves = [jnp.sum(jnp.where(own, gm[q * 2 + d], 0.0), axis=0, keepdims=True) for d in (0, 1)]
        return jnp.concatenate(halves, axis=1)

    def gather(q, carry):
        both = pl.ds(q * 2, 2)
        xs = tok[both].reshape(2 * rows, width)
        cs = cot[both].reshape(2 * rows, width)
        for e in (0, 1):
            chosen = jnp.where(gate_line(q, e) > 0.0, 1.0, 0.0)
            rank = nn(jnp.broadcast_to(chosen, (16, 2 * rows)).astype(jnp.bfloat16), earlier)[:1]
            place = jnp.where((slot == rank) & (chosen > 0.0), 1.0, 0.0).astype(jnp.bfloat16)
            pick[e, q] = place
            xrow[e, q] = nn(place, xs).astype(jnp.bfloat16)
            crow[e, q] = nn(place, cs).astype(jnp.bfloat16)
        return carry

    def gate_rows(e):
        parts = [
            jnp.sum(jnp.where(pick[e, q].astype(jnp.float32) > 0.0, gate_line(q, e), 0.0), axis=1, keepdims=True)
            for q in range(levels)
        ]
        return jnp.concatenate(parts, axis=0)

    def compute(e, base, size, first):
        units = pl.ds(pl.multiple_of(base, 16), size)
        xs = xrow[e].reshape(levels * slots, width)
        cs = crow[e].reshape(levels * slots, width)
        g = gate_rows(e)
        gate_pre = nt(xs, win[e, 0, units])
        up_pre = nt(xs, win[e, 1, units])
        gh = nt(cs, wd[e, units])
        s = jax.nn.sigmoid(gate_pre)
        act = gate_pre * s
        hidden = act * up_pre
        val = jnp.sum(hidden * gh, axis=1, keepdims=True)
        out = nn((hidden * g).astype(jnp.bfloat16), wd[e, units])
        gh = gh * g
        grad_gate = (gh * up_pre * s * (1.0 + gate_pre * (1.0 - s))).astype(jnp.bfloat16)
        grad = nn(grad_gate, win[e, 0, units])
        grad = grad + nn((gh * act).astype(jnp.bfloat16), win[e, 1, units])
        for ref, new in ((orow, out), (drow, grad), (vrow, jnp.broadcast_to(val, (levels * slots, rows)))):
            new = new.reshape(ref.shape)
            if first:
                ref[...] = new
            else:
                ref[...] += new

    def scatter(q, e, first):
        place = pick[e, q]
        out = tn(place, orow[q].astype(jnp.bfloat16)).reshape(2, rows, width)
        grad = tn(place, drow[q].astype(jnp.bfloat16)).reshape(2, rows, width)
        line = jnp.where(place.astype(jnp.float32) > 0.0, vrow[q][:, :1], 0.0)
        line = jnp.sum(line, axis=0, keepdims=True)
        own = expert_row == ex * win.shape[0] + e
        for d in (0, 1):
            gval = jnp.where(own, line[:, d * rows : (d + 1) * rows], 0.0)
            if first:
                acc[q, d, 0] = out[d]
                acc[q, d, 1] = grad[d]
                gacc[q, d] = gval
            else:
                acc[q, d, 0] += out[d]
                acc[q, d, 1] += grad[d]
                gacc[q, d] += gval

    def first_scatter(q, carry):
        scatter(q, 0, True)
        return carry

    lax.fori_loop(0, levels, gather, 0)
    pass_on(1)
    arrived(weights_forward(0, 0) + weights_forward(0, 1))
    compute(0, 0, win.shape[2], True)
    lax.fori_loop(0, levels, first_scatter, 0)
    compute(1, y * 2 * part, 2 * part, True)
    compute(1, dp_y * part, part, False)
    arrived(weights_forward(1, 0) + weights_forward(1, 1))
    compute(1, ((1 - y) * 2 + 1 - x) * part, part, False)

    def level_at(k):
        tables = ((3, 2, 1, 0), (3, 0, 2, 1), (0, 3, 1, 2), (0, 1, 2, 3))
        if levels == 2:
            tables = ((1, 0), (0, 1))
        q = jnp.int32(0)
        for i, table in enumerate(tables):
            for j, level in enumerate(table):
                q = q + jnp.where((z == i) & (k == j), level, 0)
        return q

    def to_sibling(q):
        return [
            remote(sibs.at[q, h], sibr.at[q, h], sb_ss.at[q, h], sb_rs.at[q, h], sibling) for h in (0, 1)
        ] + [remote(gsibs.at[q], gsibr.at[q], sb_ss.at[q, 2], sb_rs.at[q, 2], sibling)]

    def chain(q, direction):
        peer = below if direction else above
        dst, gdst = (dn, gdn) if direction else (up, gup)
        rs = dn_rs if direction else up_rs
        return [
            remote(snd.at[q, h], dst.at[q, h], ch_ss.at[q, h], rs.at[q, h], peer) for h in (0, 1)
        ] + [remote(gsnd.at[q], gdst.at[q], ch_ss.at[q, 2], rs.at[q, 2], peer)]

    def produce(k):
        q = level_at(k)
        scatter(q, 1, False)
        other = 1 - c
        sibs[q] = acc[q, other].astype(sibs.dtype)
        gsibs[q] = gacc[q, other]
        start(to_sibling(q))

    def take(q, direction, h):
        src, gsrc = (dn, gdn) if direction else (up, gup)
        copies = chain(q, direction)
        copies[h].wait_recv()
        acc[q, c, h] += src[q, h].astype(jnp.float32)
        if h:
            copies[2].wait_recv()
            gsnd[q] += gsrc[q]

    def hand_on(q, direction, h):
        @pl.when(has_above if direction else has_below)
        def _():
            take(q, direction, h)

        copies = chain(q, direction)
        snd[q, h] = acc[q, c, h].astype(snd.dtype)
        copies[h].start()
        if h:
            copies[2].start()

    def consume(k, h):
        q = level_at(k)
        copies = to_sibling(q)
        copies[h].wait_recv()
        acc[q, c, h] += sibr[q, h].astype(jnp.float32)
        if h:
            copies[2].wait_recv()
            gsnd[q] = gacc[q, c] + gsibr[q]

        @pl.when(q > z)
        def _():
            hand_on(q, 0, h)

        @pl.when(q < z)
        def _():
            hand_on(q, 1, h)

    def turn(k, carry):
        produce(k)

        @pl.when(k == 1)
        def _():
            consume(0, 0)
            consume(0, 1)

        return carry

    lax.fori_loop(0, levels, turn, 0)
    if levels == 4:
        for h in (0, 1):
            consume(1, h)
            consume(2, h)
    for h in (0, 1):
        consume(levels - 1, h)

        @pl.when(has_below)
        def _():
            take(z, 0, h)

        @pl.when(has_above)
        def _():
            take(z, 1, h)

    out_ref[...] = acc[z, c, 0].astype(out_ref.dtype)
    grad_ref[...] = acc[z, c, 1].astype(grad_ref.dtype)
    for k in range(choices):
        named = expert_row == ids_in[k : k + 1]
        gv_ref[k : k + 1] = jnp.sum(jnp.where(named, gsnd[z], 0.0), axis=0, keepdims=True)

    for e in (0, 1):
        for axis in (0, 1):
            left(weights_direct(e, axis) + weights_forward(e, axis))
    for step in range(top):
        @pl.when(has_above & (z - step >= 0))
        def _():
            left(token_hop(step, 0, True))

        @pl.when(has_below & (z + step <= top))
        def _():
            left(token_hop(step, 1, True))

    def finish(q, carry):
        left(token_sibling(q, True))
        left(to_sibling(q))

        @pl.when(q != z)
        def _():
            left(chain(q, 0))

        return carry

    lax.fori_loop(0, levels, finish, 0)


def fused_body(tokens, expert_ids, router_gates, w_in, w_down, cotangent):
    rows, width = tokens.shape
    members = lax.axis_size("expert")
    exp_local, _, part, _ = w_in.shape
    experts = exp_local * members
    units = part * lax.axis_size("dp")
    levels = members // 2
    choices = expert_ids.shape[1]
    capacity = rows * choices // experts + 1
    slots = -(-2 * capacity // 16) * 16
    bf16, f32 = jnp.bfloat16, jnp.float32
    dma = pltpu.SemaphoreType.DMA
    vmem = pl.BlockSpec(memory_space=pltpu.VMEM)
    hbm = pl.BlockSpec(memory_space=pl.ANY)
    out, grad, gate = pl.pallas_call(
        fused_kernel,
        out_shape=(
            jax.ShapeDtypeStruct((rows, width), bf16),
            jax.ShapeDtypeStruct((rows, width), bf16),
            jax.ShapeDtypeStruct((choices, rows), f32),
        ),
        in_specs=[hbm, hbm, vmem, vmem, hbm, hbm],
        out_specs=(vmem, vmem, vmem),
        scratch_shapes=[
            pltpu.VMEM((members, rows, width), bf16),
            pltpu.VMEM((members, rows, width), bf16),
            pltpu.VMEM((members, experts, rows), f32),
            pltpu.VMEM((exp_local, 2, units, width), bf16),
            pltpu.VMEM((exp_local, units, width), bf16),
            pltpu.VMEM((levels, 2, 2, rows, width), f32),
            pltpu.VMEM((levels, 2, experts, rows), f32),
            pltpu.VMEM((exp_local, levels, slots, 2 * rows), bf16),
            pltpu.VMEM((exp_local, levels, slots, width), bf16),
            pltpu.VMEM((exp_local, levels, slots, width), bf16),
            pltpu.VMEM((levels, slots, width), f32),
            pltpu.VMEM((levels, slots, width), f32),
            pltpu.VMEM((levels, slots, rows), f32),
            pltpu.VMEM((levels, 2, rows, width), bf16),
            pltpu.VMEM((levels, 2, rows, width), bf16),
            pltpu.VMEM((levels, experts, rows), f32),
            pltpu.VMEM((levels, experts, rows), f32),
            pltpu.VMEM((levels, 2, rows, width), bf16),
            pltpu.VMEM((levels, experts, rows), f32),
            pltpu.VMEM((levels, 2, rows, width), bf16),
            pltpu.VMEM((levels, 2, rows, width), bf16),
            pltpu.VMEM((levels, experts, rows), f32),
            pltpu.VMEM((levels, experts, rows), f32),
            dma((4,)),
            dma((2, levels - 1, 3)),
            dma((2, levels - 1, 3)),
            dma((levels, 3)),
            dma((levels, 3)),
            dma((2, 2, 2)),
            dma((2, 2, 2)),
            dma((2, 2, 2)),
            dma((2, 2, 2)),
            dma((levels, 3)),
            dma((levels, 3)),
            dma((levels, 3)),
            dma((levels, 3)),
            dma((levels, 3)),
        ],
        compiler_params=pltpu.CompilerParams(
            collective_id=0, has_side_effects=True, vmem_limit_bytes=56 * 2**20
        ),
    )(tokens, cotangent, expert_ids.T, router_gates.T, w_in, w_down)
    return out, grad, gate.T


def solution(mesh):
    rows = P(("dp", "expert"), None)
    placed = (rows, rows, rows, P("expert", None, "dp", None), P("expert", "dp", None), rows)
    fits = mesh.shape["dp"] == 4 and mesh.shape["expert"] in (4, 8)
    return jax.shard_map(
        fused_body if fits else body,
        mesh=mesh, in_specs=placed, out_specs=(rows, rows, rows), check_vma=False,
    )
```

```python
import jax
import jax.numpy as jnp
from jax import lax
from jax.experimental import pallas as pl
from jax.experimental.pallas import tpu as pltpu
from jax.sharding import PartitionSpec as P

MESH = pl.DeviceIdType.MESH


def expert_terms(x, cot, ids, gates, full_in, full_down, first_expert):
    exp_local, _, hidden_width, _ = full_in.shape
    out_sum = jnp.zeros(x.shape, jnp.float32)
    grad_sum = jnp.zeros(x.shape, jnp.float32)
    gate_sum = jnp.zeros(gates.shape, jnp.float32)
    nt = (((1,), (1,)), ((), ()))
    nn = (((1,), (0,)), ((), ()))

    def dot(a, b, dims):
        return lax.dot_general(a, b, dims, preferred_element_type=jnp.float32)

    for e in range(exp_local):
        chosen = ids == first_expert + e
        g = jnp.sum(jnp.where(chosen, gates, 0.0), axis=1, keepdims=True)
        w_pair = full_in[e].reshape(2 * hidden_width, -1)
        both = dot(x, w_pair, nt)
        gate_pre, up_pre = both[:, :hidden_width], both[:, hidden_width:]
        s = jax.nn.sigmoid(gate_pre)
        act = gate_pre * s
        hidden = act * up_pre
        gh = dot(cot, full_down[e], nt)
        gate_sum += jnp.where(chosen, jnp.sum(hidden * gh, axis=1, keepdims=True), 0.0)
        out_sum += dot((hidden * g).astype(jnp.bfloat16), full_down[e], nn)
        gh = gh * g
        grad_up = (gh * act).astype(jnp.bfloat16)
        grad_gate = (gh * up_pre * s * (1.0 + gate_pre * (1.0 - s))).astype(jnp.bfloat16)
        grad_sum += dot(jnp.concatenate([grad_gate, grad_up], axis=1), w_pair, nn)
    return out_sum.astype(jnp.bfloat16), grad_sum.astype(jnp.bfloat16), gate_sum


def body(tokens, expert_ids, router_gates, w_in, w_down, cotangent):
    exp_local = w_in.shape[0]
    first_expert = lax.axis_index("expert") * exp_local
    x = lax.all_gather(tokens, "expert", axis=0, tiled=True)
    cot = lax.all_gather(cotangent, "expert", axis=0, tiled=True)
    ids = lax.all_gather(expert_ids, "expert", axis=0, tiled=True)
    gates = lax.all_gather(router_gates, "expert", axis=0, tiled=True)
    full_in = lax.all_gather(w_in, "dp", axis=2, tiled=True)
    full_down = lax.all_gather(w_down, "dp", axis=1, tiled=True)
    rows = x.shape[0]
    if rows <= 1024:
        out, grad, gate = expert_terms(x, cot, ids, gates, full_in, full_down, first_expert)
    else:
        parts = rows // 512
        out, grad, gate = lax.map(
            lambda a: expert_terms(*a, full_in, full_down, first_expert),
            tuple(v.reshape(parts, 512, v.shape[1]) for v in (x, cot, ids, gates)),
        )
        out, grad, gate = (v.reshape(rows, v.shape[2]) for v in (out, grad, gate))
    return tuple(
        lax.psum_scatter(v, "expert", scatter_dimension=0, tiled=True) for v in (out, grad, gate)
    )


def fused_kernel(
    tok_in, cot_in, ids_in, gates_in, win_in, wd_in,
    out_ref, grad_ref, gv_ref,
    tok, cot, gm, win, wd, acc, gacc, pick, xrow, crow, orow, drow, vrow, sibs, sibr, gsibs, gsibr, snd, gsnd, up, dn, gup, gdn,
    load_sem, ag_ss, ag_rs, sg_ss, sg_rs, w_ss, w_rs, f_ss, f_rs, sb_ss, sb_rs, ch_ss, up_rs, dn_rs,
):
    dp, ex = lax.axis_index("dp"), lax.axis_index("expert")
    y, x = dp // 2, dp % 2
    z, c = ex // 2, ex % 2
    dp_x, dp_y = y * 2 + (1 - x), (1 - y) * 2 + x
    sibling = (dp, z * 2 + 1 - c)
    above, below = (dp, ex + 2), (dp, ex - 2)
    x_peer, y_peer = (dp_x, ex), (dp_y, ex)
    levels = tok.shape[0] // 2
    top = levels - 1
    part = win_in.shape[2]
    rows, width = tok_in.shape
    cut = part // 32 * 16 + 16
    has_above, has_below = z < top, z > 0

    experts, choices = gm.shape[1], ids_in.shape[0]
    expert_row = lax.broadcasted_iota(jnp.int32, (experts, rows), 0)
    gm[ex] = sum(
        jnp.where(expert_row == ids_in[k : k + 1], gates_in[k : k + 1], 0.0) for k in range(choices)
    )

    barrier = pltpu.get_barrier_semaphore()
    for peer in (sibling, x_peer, y_peer):
        pl.semaphore_signal(barrier, inc=1, device_id=peer, device_id_type=MESH)

    @pl.when(has_above)
    def _():
        pl.semaphore_signal(barrier, inc=1, device_id=above, device_id_type=MESH)

    @pl.when(has_below)
    def _():
        pl.semaphore_signal(barrier, inc=1, device_id=below, device_id_type=MESH)

    pl.semaphore_wait(barrier, 3 + jnp.where(has_above, 1, 0) + jnp.where(has_below, 1, 0))

    def remote(src, dst, ss, rs, peer):
        return pltpu.make_async_remote_copy(
            src_ref=src, dst_ref=dst, send_sem=ss, recv_sem=rs, device_id=peer, device_id_type=MESH
        )

    def unit_rows(s):
        return pl.ds(pl.multiple_of(s * part, 16), part)

    def weights_direct(e, axis):
        peer = (x_peer, y_peer)[axis]
        mine = unit_rows(dp)
        return [
            remote(win_in.at[e], win.at[e, :, mine], w_ss.at[e, axis, 0], w_rs.at[e, axis, 0], peer),
            remote(wd_in.at[e], wd.at[e, mine], w_ss.at[e, axis, 1], w_rs.at[e, axis, 1], peer),
        ]

    def weights_forward(e, axis):
        peer = (x_peer, y_peer)[axis]
        s = (dp_y, dp_x)[axis]
        base = pl.multiple_of(s * part, 16)
        mats = win.at[e, axis, unit_rows(s)]
        down = wd.at[e, pl.ds(base, cut)] if axis == 0 else wd.at[e, pl.ds(base + cut, part - cut)]
        return [
            remote(mats, mats, f_ss.at[e, axis, 0], f_rs.at[e, axis, 0], peer),
            remote(down, down, f_ss.at[e, axis, 1], f_rs.at[e, axis, 1], peer),
        ]

    def token_hop(step, direction, own):
        src = ex + 2 * step if direction else ex - 2 * step
        peer = below if direction else above
        refs = (tok, cot, gm)
        srcs = (tok_in, cot_in, gm.at[src]) if own else [r.at[src] for r in refs]
        return [
            remote(a, r.at[src], ag_ss.at[direction, step, i], ag_rs.at[direction, step, i], peer)
            for i, (a, r) in enumerate(zip(srcs, refs))
        ]

    def token_sibling(level, own=False):
        refs = (tok, cot, gm)
        src = level * 2 + c
        srcs = (tok_in, cot_in, gm.at[src]) if own else [r.at[src] for r in refs]
        return [
            remote(a, r.at[src], sg_ss.at[level, i], sg_rs.at[level, i], sibling)
            for i, (a, r) in enumerate(zip(srcs, refs))
        ]

    def start(copies):
        for copy in copies:
            copy.start()

    def arrived(copies):
        for copy in copies:
            copy.wait_recv()

    def left(copies):
        for copy in copies:
            copy.wait_send()

    start(weights_direct(0, 0) + weights_direct(0, 1))

    @pl.when(has_above)
    def _():
        start(token_hop(0, 0, True))

    @pl.when(has_below)
    def _():
        start(token_hop(0, 1, True))

    start(token_sibling(z, True))
    mine = unit_rows(dp)
    loads = [
        pltpu.make_async_copy(a, b, load_sem.at[i])
        for i, (a, b) in enumerate(
            (
                (tok_in, tok.at[ex]),
                (cot_in, cot.at[ex]),
                (win_in, win.at[:, :, mine]),
                (wd_in, wd.at[:, mine]),
            )
        )
    ]
    for load in loads:
        load.start()

    def token_step(step):
        @pl.when(z - step - 1 >= 0)
        def _():
            arrived(token_hop(step, 0, True))
            if step + 1 < top:
                @pl.when(has_above)
                def _():
                    start(token_hop(step + 1, 0, False))
            start(token_sibling(z - step - 1))

        @pl.when(z + step + 1 <= top)
        def _():
            arrived(token_hop(step, 1, True))
            if step + 1 < top:
                @pl.when(has_below)
                def _():
                    start(token_hop(step + 1, 1, False))
            start(token_sibling(z + step + 1))

    def pass_on(e):
        arrived(weights_direct(e, 0))
        start(weights_forward(e, 1))
        arrived(weights_direct(e, 1))
        start(weights_forward(e, 0))

    token_step(0)
    start(weights_direct(1, 0) + weights_direct(1, 1))
    pass_on(0)
    for step in range(1, top):
        token_step(step)
    for load in loads:
        load.wait()

    def sibling_arrival(level, carry):
        arrived(token_sibling(level, True))
        return carry

    lax.fori_loop(0, levels, sibling_arrival, 0)
    def nt(a, b):
        return lax.dot_general(a, b, (((1,), (1,)), ((), ())), preferred_element_type=jnp.float32)

    def nn(a, b):
        return lax.dot_general(a, b, (((1,), (0,)), ((), ())), preferred_element_type=jnp.float32)

    def tn(a, b):
        return lax.dot_general(a, b, (((0,), (0,)), ((), ())), preferred_element_type=jnp.float32)

    slots = pick.shape[2]
    span = (2 * rows, 2 * rows)
    earlier = lax.broadcasted_iota(jnp.int32, span, 0) < lax.broadcasted_iota(jnp.int32, span, 1)
    earlier = jnp.where(earlier, 1.0, 0.0).astype(jnp.bfloat16)
    slot = lax.broadcasted_iota(jnp.int32, (slots, 2 * rows), 0).astype(jnp.float32)

    def gate_line(q, e):
        own = expert_row == ex * win.shape[0] + e
        halves = [jnp.sum(jnp.where(own, gm[q * 2 + d], 0.0), axis=0, keepdims=True) for d in (0, 1)]
        return jnp.concatenate(halves, axis=1)

    def gather(q, carry):
        both = pl.ds(q * 2, 2)
        xs = tok[both].reshape(2 * rows, width)
        cs = cot[both].reshape(2 * rows, width)
        for e in (0, 1):
            chosen = jnp.where(gate_line(q, e) > 0.0, 1.0, 0.0)
            rank = nn(jnp.broadcast_to(chosen, (16, 2 * rows)).astype(jnp.bfloat16), earlier)[:1]
            place = jnp.where((slot == rank) & (chosen > 0.0), 1.0, 0.0).astype(jnp.bfloat16)
            pick[e, q] = place
            xrow[e, q] = nn(place, xs).astype(jnp.bfloat16)
            crow[e, q] = nn(place, cs).astype(jnp.bfloat16)
        return carry

    def gate_rows(e):
        parts = [
            jnp.sum(jnp.where(pick[e, q].astype(jnp.float32) > 0.0, gate_line(q, e), 0.0), axis=1, keepdims=True)
            for q in range(levels)
        ]
        return jnp.concatenate(parts, axis=0)

    def compute(e, base, size, first):
        units = pl.ds(pl.multiple_of(base, 16), size)
        xs = xrow[e].reshape(levels * slots, width)
        cs = crow[e].reshape(levels * slots, width)
        g = gate_rows(e)
        gate_pre = nt(xs, win[e, 0, units])
        up_pre = nt(xs, win[e, 1, units])
        gh = nt(cs, wd[e, units])
        s = jax.nn.sigmoid(gate_pre)
        act = gate_pre * s
        hidden = act * up_pre
        val = jnp.sum(hidden * gh, axis=1, keepdims=True)
        out = nn((hidden * g).astype(jnp.bfloat16), wd[e, units])
        gh = gh * g
        grad_gate = (gh * up_pre * s * (1.0 + gate_pre * (1.0 - s))).astype(jnp.bfloat16)
        grad = nn(grad_gate, win[e, 0, units])
        grad = grad + nn((gh * act).astype(jnp.bfloat16), win[e, 1, units])
        for ref, new in ((orow, out), (drow, grad), (vrow, jnp.broadcast_to(val, (levels * slots, rows)))):
            new = new.reshape(ref.shape)
            if first:
                ref[...] = new
            else:
                ref[...] += new

    def scatter(q, e, first):
        place = pick[e, q]
        out = tn(place, orow[q].astype(jnp.bfloat16)).reshape(2, rows, width)
        grad = tn(place, drow[q].astype(jnp.bfloat16)).reshape(2, rows, width)
        line = jnp.where(place.astype(jnp.float32) > 0.0, vrow[q][:, :1], 0.0)
        line = jnp.sum(line, axis=0, keepdims=True)
        own = expert_row == ex * win.shape[0] + e
        for d in (0, 1):
            gval = jnp.where(own, line[:, d * rows : (d + 1) * rows], 0.0)
            if first:
                acc[q, d, 0] = out[d]
                acc[q, d, 1] = grad[d]
                gacc[q, d] = gval
            else:
                acc[q, d, 0] += out[d]
                acc[q, d, 1] += grad[d]
                gacc[q, d] += gval

    def first_scatter(q, carry):
        scatter(q, 0, True)
        return carry

    lax.fori_loop(0, levels, gather, 0)
    pass_on(1)
    arrived(weights_forward(0, 0) + weights_forward(0, 1))
    compute(0, 0, win.shape[2], True)
    lax.fori_loop(0, levels, first_scatter, 0)
    compute(1, y * 2 * part, 2 * part, True)
    compute(1, dp_y * part, part, False)
    arrived(weights_forward(1, 0) + weights_forward(1, 1))
    compute(1, ((1 - y) * 2 + 1 - x) * part, part, False)

    def level_at(k):
        tables = ((3, 2, 1, 0), (3, 0, 2, 1), (0, 3, 1, 2), (0, 1, 2, 3))
        if levels == 2:
            tables = ((1, 0), (0, 1))
        q = jnp.int32(0)
        for i, table in enumerate(tables):
            for j, level in enumerate(table):
                q = q + jnp.where((z == i) & (k == j), level, 0)
        return q

    def to_sibling(q):
        return [
            remote(sibs.at[q, h], sibr.at[q, h], sb_ss.at[q, h], sb_rs.at[q, h], sibling) for h in (0, 1)
        ] + [remote(gsibs.at[q], gsibr.at[q], sb_ss.at[q, 2], sb_rs.at[q, 2], sibling)]

    def chain(q, direction):
        peer = below if direction else above
        dst, gdst = (dn, gdn) if direction else (up, gup)
        rs = dn_rs if direction else up_rs
        return [
            remote(snd.at[q, h], dst.at[q, h], ch_ss.at[q, h], rs.at[q, h], peer) for h in (0, 1)
        ] + [remote(gsnd.at[q], gdst.at[q], ch_ss.at[q, 2], rs.at[q, 2], peer)]

    def produce(k):
        q = level_at(k)
        scatter(q, 1, False)
        other = 1 - c
        sibs[q] = acc[q, other].astype(sibs.dtype)
        gsibs[q] = gacc[q, other]
        start(to_sibling(q))

    def take(q, direction, h):
        src, gsrc = (dn, gdn) if direction else (up, gup)
        copies = chain(q, direction)
        copies[h].wait_recv()
        acc[q, c, h] += src[q, h].astype(jnp.float32)
        if h:
            copies[2].wait_recv()
            gsnd[q] += gsrc[q]

    def hand_on(q, direction, h):
        @pl.when(has_above if direction else has_below)
        def _():
            take(q, direction, h)

        copies = chain(q, direction)
        snd[q, h] = acc[q, c, h].astype(snd.dtype)
        copies[h].start()
        if h:
            copies[2].start()

    def consume(k, h):
        q = level_at(k)
        copies = to_sibling(q)
        copies[h].wait_recv()
        acc[q, c, h] += sibr[q, h].astype(jnp.float32)
        if h:
            copies[2].wait_recv()
            gsnd[q] = gacc[q, c] + gsibr[q]

        @pl.when(q > z)
        def _():
            hand_on(q, 0, h)

        @pl.when(q < z)
        def _():
            hand_on(q, 1, h)

    def turn(k, carry):
        produce(k)

        @pl.when(k == 1)
        def _():
            consume(0, 0)
            consume(0, 1)

        return carry

    lax.fori_loop(0, levels, turn, 0)
    if levels == 4:
        for h in (0, 1):
            consume(1, h)
            consume(2, h)
    for h in (0, 1):
        consume(levels - 1, h)

        @pl.when(has_below)
        def _():
            take(z, 0, h)

        @pl.when(has_above)
        def _():
            take(z, 1, h)

    out_ref[...] = acc[z, c, 0].astype(out_ref.dtype)
    grad_ref[...] = acc[z, c, 1].astype(grad_ref.dtype)
    for k in range(choices):
        named = expert_row == ids_in[k : k + 1]
        gv_ref[k : k + 1] = jnp.sum(jnp.where(named, gsnd[z], 0.0), axis=0, keepdims=True)

    for e in (0, 1):
        for axis in (0, 1):
            left(weights_direct(e, axis) + weights_forward(e, axis))
    for step in range(top):
        @pl.when(has_above & (z - step >= 0))
        def _():
            left(token_hop(step, 0, True))

        @pl.when(has_below & (z + step <= top))
        def _():
            left(token_hop(step, 1, True))

    def finish(q, carry):
        left(token_sibling(q, True))
        left(to_sibling(q))

        @pl.when(q != z)
        def _():
            left(chain(q, 0))

        return carry

    lax.fori_loop(0, levels, finish, 0)


def fused_body(tokens, expert_ids, router_gates, w_in, w_down, cotangent):
    rows, width = tokens.shape
    members = lax.axis_size("expert")
    exp_local, _, part, _ = w_in.shape
    experts = exp_local * members
    units = part * lax.axis_size("dp")
    levels = members // 2
    choices = expert_ids.shape[1]
    capacity = rows * choices // experts + 1
    slots = -(-2 * capacity // 16) * 16
    bf16, f32 = jnp.bfloat16, jnp.float32
    dma = pltpu.SemaphoreType.DMA
    vmem = pl.BlockSpec(memory_space=pltpu.VMEM)
    hbm = pl.BlockSpec(memory_space=pl.ANY)
    out, grad, gate = pl.pallas_call(
        fused_kernel,
        out_shape=(
            jax.ShapeDtypeStruct((rows, width), f32),
            jax.ShapeDtypeStruct((rows, width), f32),
            jax.ShapeDtypeStruct((choices, rows), f32),
        ),
        in_specs=[hbm, hbm, vmem, vmem, hbm, hbm],
        out_specs=(vmem, vmem, vmem),
        scratch_shapes=[
            pltpu.VMEM((members, rows, width), bf16),
            pltpu.VMEM((members, rows, width), bf16),
            pltpu.VMEM((members, experts, rows), f32),
            pltpu.VMEM((exp_local, 2, units, width), bf16),
            pltpu.VMEM((exp_local, units, width), bf16),
            pltpu.VMEM((levels, 2, 2, rows, width), f32),
            pltpu.VMEM((levels, 2, experts, rows), f32),
            pltpu.VMEM((exp_local, levels, slots, 2 * rows), bf16),
            pltpu.VMEM((exp_local, levels, slots, width), bf16),
            pltpu.VMEM((exp_local, levels, slots, width), bf16),
            pltpu.VMEM((levels, slots, width), f32),
            pltpu.VMEM((levels, slots, width), f32),
            pltpu.VMEM((levels, slots, rows), f32),
            pltpu.VMEM((levels, 2, rows, width), bf16),
            pltpu.VMEM((levels, 2, rows, width), bf16),
            pltpu.VMEM((levels, experts, rows), f32),
            pltpu.VMEM((levels, experts, rows), f32),
            pltpu.VMEM((levels, 2, rows, width), bf16),
            pltpu.VMEM((levels, experts, rows), f32),
            pltpu.VMEM((levels, 2, rows, width), bf16),
            pltpu.VMEM((levels, 2, rows, width), bf16),
            pltpu.VMEM((levels, experts, rows), f32),
            pltpu.VMEM((levels, experts, rows), f32),
            dma((4,)),
            dma((2, levels - 1, 3)),
            dma((2, levels - 1, 3)),
            dma((levels, 3)),
            dma((levels, 3)),
            dma((2, 2, 2)),
            dma((2, 2, 2)),
            dma((2, 2, 2)),
            dma((2, 2, 2)),
            dma((levels, 3)),
            dma((levels, 3)),
            dma((levels, 3)),
            dma((levels, 3)),
            dma((levels, 3)),
        ],
        compiler_params=pltpu.CompilerParams(
            collective_id=0, has_side_effects=True, vmem_limit_bytes=56 * 2**20
        ),
    )(tokens, cotangent, expert_ids.T, router_gates.T, w_in, w_down)
    return out.astype(bf16), grad.astype(bf16), gate.T


def solution(mesh):
    rows = P(("dp", "expert"), None)
    placed = (rows, rows, rows, P("expert", None, "dp", None), P("expert", "dp", None), rows)
    fits = mesh.shape["dp"] == 4 and mesh.shape["expert"] in (4, 8)
    return jax.shard_map(
        fused_body if fits else body,
        mesh=mesh, in_specs=placed, out_specs=(rows, rows, rows), check_vma=False,
    )
```

```python
import jax
import jax.numpy as jnp
from jax import lax
from jax.experimental import pallas as pl
from jax.experimental.pallas import tpu as pltpu
from jax.sharding import PartitionSpec as P

MESH = pl.DeviceIdType.MESH


def expert_terms(x, cot, ids, gates, full_in, full_down, first_expert):
    exp_local, _, hidden_width, _ = full_in.shape
    out_sum = jnp.zeros(x.shape, jnp.float32)
    grad_sum = jnp.zeros(x.shape, jnp.float32)
    gate_sum = jnp.zeros(gates.shape, jnp.float32)
    nt = (((1,), (1,)), ((), ()))
    nn = (((1,), (0,)), ((), ()))

    def dot(a, b, dims):
        return lax.dot_general(a, b, dims, preferred_element_type=jnp.float32)

    for e in range(exp_local):
        chosen = ids == first_expert + e
        g = jnp.sum(jnp.where(chosen, gates, 0.0), axis=1, keepdims=True)
        w_pair = full_in[e].reshape(2 * hidden_width, -1)
        both = dot(x, w_pair, nt)
        gate_pre, up_pre = both[:, :hidden_width], both[:, hidden_width:]
        s = jax.nn.sigmoid(gate_pre)
        act = gate_pre * s
        hidden = act * up_pre
        gh = dot(cot, full_down[e], nt)
        gate_sum += jnp.where(chosen, jnp.sum(hidden * gh, axis=1, keepdims=True), 0.0)
        out_sum += dot((hidden * g).astype(jnp.bfloat16), full_down[e], nn)
        gh = gh * g
        grad_up = (gh * act).astype(jnp.bfloat16)
        grad_gate = (gh * up_pre * s * (1.0 + gate_pre * (1.0 - s))).astype(jnp.bfloat16)
        grad_sum += dot(jnp.concatenate([grad_gate, grad_up], axis=1), w_pair, nn)
    return out_sum.astype(jnp.bfloat16), grad_sum.astype(jnp.bfloat16), gate_sum


def body(tokens, expert_ids, router_gates, w_in, w_down, cotangent):
    exp_local = w_in.shape[0]
    first_expert = lax.axis_index("expert") * exp_local
    x = lax.all_gather(tokens, "expert", axis=0, tiled=True)
    cot = lax.all_gather(cotangent, "expert", axis=0, tiled=True)
    ids = lax.all_gather(expert_ids, "expert", axis=0, tiled=True)
    gates = lax.all_gather(router_gates, "expert", axis=0, tiled=True)
    full_in = lax.all_gather(w_in, "dp", axis=2, tiled=True)
    full_down = lax.all_gather(w_down, "dp", axis=1, tiled=True)
    rows = x.shape[0]
    if rows <= 1024:
        out, grad, gate = expert_terms(x, cot, ids, gates, full_in, full_down, first_expert)
    else:
        parts = rows // 512
        out, grad, gate = lax.map(
            lambda a: expert_terms(*a, full_in, full_down, first_expert),
            tuple(v.reshape(parts, 512, v.shape[1]) for v in (x, cot, ids, gates)),
        )
        out, grad, gate = (v.reshape(rows, v.shape[2]) for v in (out, grad, gate))
    return tuple(
        lax.psum_scatter(v, "expert", scatter_dimension=0, tiled=True) for v in (out, grad, gate)
    )


def fused_kernel(
    tok_in, cot_in, ids_in, gates_in, win_in, wd_in,
    out_ref, grad_ref, gv_ref,
    tok, cot, gm, win, wd, acc, gacc, pick, xrow, crow, orow, drow, vrow, sibs, sibr, gsibs, gsibr, snd, gsnd, up, dn, gup, gdn,
    load_sem, ag_ss, ag_rs, sg_ss, sg_rs, w_ss, w_rs, f_ss, f_rs, sb_ss, sb_rs, ch_ss, up_rs, dn_rs,
):
    dp, ex = lax.axis_index("dp"), lax.axis_index("expert")
    y, x = dp // 2, dp % 2
    z, c = ex // 2, ex % 2
    dp_x, dp_y = y * 2 + (1 - x), (1 - y) * 2 + x
    sibling = (dp, z * 2 + 1 - c)
    above, below = (dp, ex + 2), (dp, ex - 2)
    x_peer, y_peer = (dp_x, ex), (dp_y, ex)
    levels = tok.shape[0] // 2
    top = levels - 1
    part = win_in.shape[2]
    rows, width = tok_in.shape
    cut = part // 32 * 16 + 16
    has_above, has_below = z < top, z > 0

    experts, choices = gm.shape[1], ids_in.shape[0]
    expert_row = lax.broadcasted_iota(jnp.int32, (experts, rows), 0)
    gm[ex] = sum(
        jnp.where(expert_row == ids_in[k : k + 1], gates_in[k : k + 1], 0.0) for k in range(choices)
    )

    barrier = pltpu.get_barrier_semaphore()
    for peer in (sibling, x_peer, y_peer):
        pl.semaphore_signal(barrier, inc=1, device_id=peer, device_id_type=MESH)

    @pl.when(has_above)
    def _():
        pl.semaphore_signal(barrier, inc=1, device_id=above, device_id_type=MESH)

    @pl.when(has_below)
    def _():
        pl.semaphore_signal(barrier, inc=1, device_id=below, device_id_type=MESH)

    pl.semaphore_wait(barrier, 3 + jnp.where(has_above, 1, 0) + jnp.where(has_below, 1, 0))

    def remote(src, dst, ss, rs, peer):
        return pltpu.make_async_remote_copy(
            src_ref=src, dst_ref=dst, send_sem=ss, recv_sem=rs, device_id=peer, device_id_type=MESH
        )

    def unit_rows(s):
        return pl.ds(pl.multiple_of(s * part, 16), part)

    def weights_direct(e, axis):
        peer = (x_peer, y_peer)[axis]
        mine = unit_rows(dp)
        return [
            remote(win_in.at[e], win.at[e, :, mine], w_ss.at[e, axis, 0], w_rs.at[e, axis, 0], peer),
            remote(wd_in.at[e], wd.at[e, mine], w_ss.at[e, axis, 1], w_rs.at[e, axis, 1], peer),
        ]

    def weights_forward(e, axis):
        peer = (x_peer, y_peer)[axis]
        s = (dp_y, dp_x)[axis]
        base = pl.multiple_of(s * part, 16)
        mats = win.at[e, axis, unit_rows(s)]
        down = wd.at[e, pl.ds(base, cut)] if axis == 0 else wd.at[e, pl.ds(base + cut, part - cut)]
        return [
            remote(mats, mats, f_ss.at[e, axis, 0], f_rs.at[e, axis, 0], peer),
            remote(down, down, f_ss.at[e, axis, 1], f_rs.at[e, axis, 1], peer),
        ]

    def token_hop(step, direction, own):
        src = ex + 2 * step if direction else ex - 2 * step
        peer = below if direction else above
        refs = (tok, cot, gm)
        srcs = (tok_in, cot_in, gm.at[src]) if own else [r.at[src] for r in refs]
        return [
            remote(a, r.at[src], ag_ss.at[direction, step, i], ag_rs.at[direction, step, i], peer)
            for i, (a, r) in enumerate(zip(srcs, refs))
        ]

    def token_sibling(level, own=False):
        refs = (tok, cot, gm)
        src = level * 2 + c
        srcs = (tok_in, cot_in, gm.at[src]) if own else [r.at[src] for r in refs]
        return [
            remote(a, r.at[src], sg_ss.at[level, i], sg_rs.at[level, i], sibling)
            for i, (a, r) in enumerate(zip(srcs, refs))
        ]

    def start(copies):
        for copy in copies:
            copy.start()

    def arrived(copies):
        for copy in copies:
            copy.wait_recv()

    def left(copies):
        for copy in copies:
            copy.wait_send()

    start(weights_direct(0, 0) + weights_direct(0, 1))

    @pl.when(has_above)
    def _():
        start(token_hop(0, 0, True))

    @pl.when(has_below)
    def _():
        start(token_hop(0, 1, True))

    start(token_sibling(z, True))
    mine = unit_rows(dp)
    loads = [
        pltpu.make_async_copy(a, b, load_sem.at[i])
        for i, (a, b) in enumerate(
            (
                (tok_in, tok.at[ex]),
                (cot_in, cot.at[ex]),
                (win_in, win.at[:, :, mine]),
                (wd_in, wd.at[:, mine]),
            )
        )
    ]
    for load in loads:
        load.start()

    def token_step(step):
        @pl.when(z - step - 1 >= 0)
        def _():
            arrived(token_hop(step, 0, True))
            if step + 1 < top:
                @pl.when(has_above)
                def _():
                    start(token_hop(step + 1, 0, False))
            start(token_sibling(z - step - 1))

        @pl.when(z + step + 1 <= top)
        def _():
            arrived(token_hop(step, 1, True))
            if step + 1 < top:
                @pl.when(has_below)
                def _():
                    start(token_hop(step + 1, 1, False))
            start(token_sibling(z + step + 1))

    def pass_on(e):
        for i in (0, 1):
            for axis in (0, 1):
                weights_direct(e, axis)[i].wait_recv()
                weights_forward(e, 1 - axis)[i].start()

    token_step(0)
    start(weights_direct(1, 0) + weights_direct(1, 1))
    pass_on(0)
    for step in range(1, top):
        token_step(step)
    for load in loads:
        load.wait()

    def sibling_arrival(level, carry):
        arrived(token_sibling(level, True))
        return carry

    lax.fori_loop(0, levels, sibling_arrival, 0)
    def nt(a, b):
        return lax.dot_general(a, b, (((1,), (1,)), ((), ())), preferred_element_type=jnp.float32)

    def nn(a, b):
        return lax.dot_general(a, b, (((1,), (0,)), ((), ())), preferred_element_type=jnp.float32)

    def tn(a, b):
        return lax.dot_general(a, b, (((0,), (0,)), ((), ())), preferred_element_type=jnp.float32)

    slots = pick.shape[2]
    span = (2 * rows, 2 * rows)
    earlier = lax.broadcasted_iota(jnp.int32, span, 0) < lax.broadcasted_iota(jnp.int32, span, 1)
    earlier = jnp.where(earlier, 1.0, 0.0).astype(jnp.bfloat16)
    slot = lax.broadcasted_iota(jnp.int32, (slots, 2 * rows), 0).astype(jnp.float32)

    def gate_line(q, e):
        own = expert_row == ex * win.shape[0] + e
        halves = [jnp.sum(jnp.where(own, gm[q * 2 + d], 0.0), axis=0, keepdims=True) for d in (0, 1)]
        return jnp.concatenate(halves, axis=1)

    def gather(q, carry):
        both = pl.ds(q * 2, 2)
        xs = tok[both].reshape(2 * rows, width)
        cs = cot[both].reshape(2 * rows, width)
        for e in (0, 1):
            chosen = jnp.where(gate_line(q, e) > 0.0, 1.0, 0.0)
            rank = nn(jnp.broadcast_to(chosen, (16, 2 * rows)).astype(jnp.bfloat16), earlier)[:1]
            place = jnp.where((slot == rank) & (chosen > 0.0), 1.0, 0.0).astype(jnp.bfloat16)
            pick[e, q] = place
            xrow[e, q] = nn(place, xs).astype(jnp.bfloat16)
            crow[e, q] = nn(place, cs).astype(jnp.bfloat16)
        return carry

    def gate_rows(e):
        parts = [
            jnp.sum(jnp.where(pick[e, q].astype(jnp.float32) > 0.0, gate_line(q, e), 0.0), axis=1, keepdims=True)
            for q in range(levels)
        ]
        return jnp.concatenate(parts, axis=0)

    def compute(e, base, size, first):
        units = pl.ds(pl.multiple_of(base, 16), size)
        xs = xrow[e].reshape(levels * slots, width)
        cs = crow[e].reshape(levels * slots, width)
        g = gate_rows(e)
        gate_pre = nt(xs, win[e, 0, units])
        up_pre = nt(xs, win[e, 1, units])
        gh = nt(cs, wd[e, units])
        s = jax.nn.sigmoid(gate_pre)
        act = gate_pre * s
        hidden = act * up_pre
        val = jnp.sum(hidden * gh, axis=1, keepdims=True)
        out = nn((hidden * g).astype(jnp.bfloat16), wd[e, units])
        gh = gh * g
        grad_gate = (gh * up_pre * s * (1.0 + gate_pre * (1.0 - s))).astype(jnp.bfloat16)
        grad = nn(grad_gate, win[e, 0, units])
        grad = grad + nn((gh * act).astype(jnp.bfloat16), win[e, 1, units])
        for ref, new in ((orow, out), (drow, grad), (vrow, jnp.broadcast_to(val, (levels * slots, rows)))):
            new = new.reshape(ref.shape)
            if first:
                ref[...] = new
            else:
                ref[...] += new

    def scatter(q, e, first):
        place = pick[e, q]
        out = tn(place, orow[q].astype(jnp.bfloat16)).reshape(2, rows, width)
        grad = tn(place, drow[q].astype(jnp.bfloat16)).reshape(2, rows, width)
        line = jnp.where(place.astype(jnp.float32) > 0.0, vrow[q][:, :1], 0.0)
        line = jnp.sum(line, axis=0, keepdims=True)
        own = expert_row == ex * win.shape[0] + e
        for d in (0, 1):
            gval = jnp.where(own, line[:, d * rows : (d + 1) * rows], 0.0)
            if first:
                acc[q, d, 0] = out[d]
                acc[q, d, 1] = grad[d]
                gacc[q, d] = gval
            else:
                acc[q, d, 0] += out[d]
                acc[q, d, 1] += grad[d]
                gacc[q, d] += gval

    def first_scatter(q, carry):
        scatter(q, 0, True)
        return carry

    lax.fori_loop(0, levels, gather, 0)
    pass_on(1)
    arrived(weights_forward(0, 0) + weights_forward(0, 1))
    compute(0, 0, win.shape[2], True)
    lax.fori_loop(0, levels, first_scatter, 0)
    compute(1, y * 2 * part, 2 * part, True)
    compute(1, dp_y * part, part, False)
    arrived(weights_forward(1, 0) + weights_forward(1, 1))
    compute(1, ((1 - y) * 2 + 1 - x) * part, part, False)

    def level_at(k):
        tables = ((3, 2, 1, 0), (3, 0, 2, 1), (0, 3, 1, 2), (0, 1, 2, 3))
        if levels == 2:
            tables = ((1, 0), (0, 1))
        q = jnp.int32(0)
        for i, table in enumerate(tables):
            for j, level in enumerate(table):
                q = q + jnp.where((z == i) & (k == j), level, 0)
        return q

    def to_sibling(q):
        return [
            remote(sibs.at[q, h], sibr.at[q, h], sb_ss.at[q, h], sb_rs.at[q, h], sibling) for h in (0, 1)
        ] + [remote(gsibs.at[q], gsibr.at[q], sb_ss.at[q, 2], sb_rs.at[q, 2], sibling)]

    def chain(q, direction):
        peer = below if direction else above
        dst, gdst = (dn, gdn) if direction else (up, gup)
        rs = dn_rs if direction else up_rs
        return [
            remote(snd.at[q, h], dst.at[q, h], ch_ss.at[q, h], rs.at[q, h], peer) for h in (0, 1)
        ] + [remote(gsnd.at[q], gdst.at[q], ch_ss.at[q, 2], rs.at[q, 2], peer)]

    def produce(k):
        q = level_at(k)
        scatter(q, 1, False)
        other = 1 - c
        sibs[q] = acc[q, other].astype(sibs.dtype)
        gsibs[q] = gacc[q, other]
        start(to_sibling(q))

    def take(q, direction, h):
        src, gsrc = (dn, gdn) if direction else (up, gup)
        copies = chain(q, direction)
        copies[h].wait_recv()
        acc[q, c, h] += src[q, h].astype(jnp.float32)
        if h:
            copies[2].wait_recv()
            gsnd[q] += gsrc[q]

    def hand_on(q, direction, h):
        @pl.when(has_above if direction else has_below)
        def _():
            take(q, direction, h)

        copies = chain(q, direction)
        snd[q, h] = acc[q, c, h].astype(snd.dtype)
        copies[h].start()
        if h:
            copies[2].start()

    def consume(k, h):
        q = level_at(k)
        copies = to_sibling(q)
        copies[h].wait_recv()
        acc[q, c, h] += sibr[q, h].astype(jnp.float32)
        if h:
            copies[2].wait_recv()
            gsnd[q] = gacc[q, c] + gsibr[q]

        @pl.when(q > z)
        def _():
            hand_on(q, 0, h)

        @pl.when(q < z)
        def _():
            hand_on(q, 1, h)

    def turn(k, carry):
        produce(k)

        @pl.when(k == 1)
        def _():
            consume(0, 0)
            consume(0, 1)

        return carry

    lax.fori_loop(0, levels, turn, 0)
    if levels == 4:
        for h in (0, 1):
            consume(1, h)
            consume(2, h)
    for h in (0, 1):
        consume(levels - 1, h)

        @pl.when(has_below)
        def _():
            take(z, 0, h)

        @pl.when(has_above)
        def _():
            take(z, 1, h)

    out_ref[...] = acc[z, c, 0].astype(out_ref.dtype)
    grad_ref[...] = acc[z, c, 1].astype(grad_ref.dtype)
    for k in range(choices):
        named = expert_row == ids_in[k : k + 1]
        gv_ref[k : k + 1] = jnp.sum(jnp.where(named, gsnd[z], 0.0), axis=0, keepdims=True)

    for e in (0, 1):
        for axis in (0, 1):
            left(weights_direct(e, axis) + weights_forward(e, axis))
    for step in range(top):
        @pl.when(has_above & (z - step >= 0))
        def _():
            left(token_hop(step, 0, True))

        @pl.when(has_below & (z + step <= top))
        def _():
            left(token_hop(step, 1, True))

    def finish(q, carry):
        left(token_sibling(q, True))
        left(to_sibling(q))

        @pl.when(q != z)
        def _():
            left(chain(q, 0))

        return carry

    lax.fori_loop(0, levels, finish, 0)


def fused_body(tokens, expert_ids, router_gates, w_in, w_down, cotangent):
    rows, width = tokens.shape
    members = lax.axis_size("expert")
    exp_local, _, part, _ = w_in.shape
    experts = exp_local * members
    units = part * lax.axis_size("dp")
    levels = members // 2
    choices = expert_ids.shape[1]
    capacity = rows * choices // experts + 1
    slots = -(-2 * capacity // 16) * 16
    bf16, f32 = jnp.bfloat16, jnp.float32
    dma = pltpu.SemaphoreType.DMA
    vmem = pl.BlockSpec(memory_space=pltpu.VMEM)
    hbm = pl.BlockSpec(memory_space=pl.ANY)
    out, grad, gate = pl.pallas_call(
        fused_kernel,
        out_shape=(
            jax.ShapeDtypeStruct((rows, width), bf16),
            jax.ShapeDtypeStruct((rows, width), bf16),
            jax.ShapeDtypeStruct((choices, rows), f32),
        ),
        in_specs=[hbm, hbm, vmem, vmem, hbm, hbm],
        out_specs=(vmem, vmem, vmem),
        scratch_shapes=[
            pltpu.VMEM((members, rows, width), bf16),
            pltpu.VMEM((members, rows, width), bf16),
            pltpu.VMEM((members, experts, rows), f32),
            pltpu.VMEM((exp_local, 2, units, width), bf16),
            pltpu.VMEM((exp_local, units, width), bf16),
            pltpu.VMEM((levels, 2, 2, rows, width), f32),
            pltpu.VMEM((levels, 2, experts, rows), f32),
            pltpu.VMEM((exp_local, levels, slots, 2 * rows), bf16),
            pltpu.VMEM((exp_local, levels, slots, width), bf16),
            pltpu.VMEM((exp_local, levels, slots, width), bf16),
            pltpu.VMEM((levels, slots, width), f32),
            pltpu.VMEM((levels, slots, width), f32),
            pltpu.VMEM((levels, slots, rows), f32),
            pltpu.VMEM((levels, 2, rows, width), bf16),
            pltpu.VMEM((levels, 2, rows, width), bf16),
            pltpu.VMEM((levels, experts, rows), f32),
            pltpu.VMEM((levels, experts, rows), f32),
            pltpu.VMEM((levels, 2, rows, width), bf16),
            pltpu.VMEM((levels, experts, rows), f32),
            pltpu.VMEM((levels, 2, rows, width), bf16),
            pltpu.VMEM((levels, 2, rows, width), bf16),
            pltpu.VMEM((levels, experts, rows), f32),
            pltpu.VMEM((levels, experts, rows), f32),
            dma((4,)),
            dma((2, levels - 1, 3)),
            dma((2, levels - 1, 3)),
            dma((levels, 3)),
            dma((levels, 3)),
            dma((2, 2, 2)),
            dma((2, 2, 2)),
            dma((2, 2, 2)),
            dma((2, 2, 2)),
            dma((levels, 3)),
            dma((levels, 3)),
            dma((levels, 3)),
            dma((levels, 3)),
            dma((levels, 3)),
        ],
        compiler_params=pltpu.CompilerParams(
            collective_id=0, has_side_effects=True, vmem_limit_bytes=56 * 2**20
        ),
    )(tokens, cotangent, expert_ids.T, router_gates.T, w_in, w_down)
    return out, grad, gate.T


def solution(mesh):
    rows = P(("dp", "expert"), None)
    placed = (rows, rows, rows, P("expert", None, "dp", None), P("expert", "dp", None), rows)
    fits = mesh.shape["dp"] == 4 and mesh.shape["expert"] in (4, 8)
    return jax.shard_map(
        fused_body if fits else body,
        mesh=mesh, in_specs=placed, out_specs=(rows, rows, rows), check_vma=False,
    )
```
